256 devices in a mesh: inst: 32 (over y, x, core), space: 8 (over z).
Axes of the slice: x: 4, y: 4, z: 8, core: 2. Of those that a mesh axis runs over, the one named last changes fastest.
Arguments:
- harmonic_state: bfloat16 [32, 122880], P('inst', 'space'), may hold values from -6 to 6
- direction: bfloat16 [32, 122880], P('inst', 'space'), may hold values from -6 to 6
- source: float32 [32, 122880], P('inst', 'space'), may hold values from -6 to 6
- jacobian: bfloat16 [32, 384, 102400], P('inst', 'space'), may hold values from -0.3125 to 0.3125
- frequency: float32 [1], replicated, may hold values from 0.05 to 0.2
- viscosity: float32 [1], replicated, may hold values from 0.01 to 0.03
- quad_weight: float32 [16], replicated, may hold values from 0.3 to 3
- partner_device: int32 [32, 1536, 1], P('inst', 'space'), may hold values from 0 to 7; in each aligned block of 192 rows (0 to 191, 192 to 383, ..., all dimensions but the last counted through in order) at most 96 rows name the same one
- partner_face: int32 [32, 1536], P('inst', 'space'), may hold values from 0 to 287
- local_face: int32 [32, 1536], P('inst', 'space'), may hold values from 0 to 287
- weight_index: int32 [32, 1536], P('inst', 'space'), may hold values from 0 to 15
Outputs:
- residual: float32 [32, 122880], P('inst', 'space')
- product: float32 [32, 122880], P('inst', 'space')
The draws below stay inside these ranges and needn't reach their ends.
Inputs may be any that keep to these rules, and one draw needn't show every extreme that they name: `partner_device`: within the 192 slots of one device, each partner device is named at most 96 times, and some device is named exactly 96 times in every draw.
All inputs are finite; a program needn't handle non-finite values.
Results may differ from the reference program's by a relative error of at most 0.00035.
Values may be sent and summed in bfloat16 or wider, within the bound.
No kernel may reach another device: no remote copies, remote signals or barrier semaphores. Data moves between devices by JAX's collectives and lax.ppermute only.
A program may use at most 64 MiB of HBM per device.

```python
import math
import jax
import jax.numpy as jnp
import numpy as np
from jax import lax

VARS = 5
PNODE = 4
NQ = 16
NT = 32
DOF = 320
NE = 384
FACES_DEV = 288
OVL = 192
CAP = 96
SLOTS = 1536
N_SPACE = 8


def set_ends(result, key, least, high):
    longest = result.shape.index(max(result.shape))
    spots = []
    for shift in (0, 1):
        where = [jax.random.randint(jax.random.fold_in(key, axis), (), 0, length) for axis, length in enumerate(result.shape)]
        where[longest] = (where[longest] + shift) % result.shape[longest]
        spots.append(tuple(where))
    return result.at[spots[0]].set(least).at[spots[1]].set(high)


def levels(stream_key, shape, shards, smallest, largest):
    def one(dim, blocks):
        draws = jax.random.uniform(jax.random.fold_in(jax.random.fold_in(stream_key, 6), dim), (blocks,), jnp.float32, smallest / len(shards), largest / len(shards))
        return jnp.repeat(jnp.exp(draws), shape[dim] // blocks).reshape((-1,) + (1,) * (len(shape) - dim - 1))

    factor_of = one(*shards[0])
    for cut in shards[1:]:
        factor_of = factor_of * one(*cut)
    return factor_of


def deal_out(stream_key, own, number, rows, amount, top, limit, slope):
    sequence = jax.random.permutation(stream_key, amount)
    packed, ordinary = load_shares(amount, rows * top, limit, slope, True), load_shares(amount, rows * top, limit, slope, False)
    places = jnp.arange(amount)

    def named(tallies, turn):
        used = int((tallies > 0).sum())
        fixed = max(1, used // 4)
        shifted = fixed + (places - fixed + turn * (used - fixed)) % max(1, amount - fixed)
        return jnp.zeros((amount,), jnp.int32).at[sequence[jnp.where(places < fixed, places, shifted)]].set(jnp.asarray(tallies, jnp.int32))

    tallies = jnp.where(number % 4 == 0, named(packed, number // 4), named(ordinary, number - number // 4 - 1))
    mixed = jax.random.permutation(jax.random.fold_in(own, 3), amount)
    donor, taker = mixed[0:amount // 2 * 2:2], mixed[1:amount // 2 * 2:2]
    margin = jnp.minimum(tallies[donor] - 1, limit - tallies[taker]) // 2
    margin = jnp.where((donor == sequence[0]) | (taker == sequence[0]) | (tallies[taker] == 0), 0, jnp.maximum(margin, 0))
    shifted = jax.random.randint(jax.random.fold_in(own, 4), (amount // 2,), 0, 1 << 20) % (margin + 1)
    tallies = tallies.at[donor].add(-shifted).at[taker].add(shifted)
    labels = jnp.searchsorted(jnp.cumsum(tallies), jnp.arange(rows * top), side="right").astype(jnp.int32)
    grid = labels.reshape(top, rows).T
    grid = grid[jax.random.permutation(jax.random.fold_in(own, 1), rows)]
    turn = jax.random.randint(jax.random.fold_in(own, 2), (rows, 1), 0, top)
    return jnp.take_along_axis(grid, (jnp.arange(top)[None, :] + turn) % top, axis=1)


def load_shares(amount, total, bound, skew, full):
    loads = [(1 << 20) // math.isqrt(standing ** skew) + 1 for standing in range(1, amount + 1)]
    largest = bound if full else min(bound, max(-(-total // amount), total * loads[0] // sum(loads)))
    least = 1 if total - largest >= amount - 1 else 0
    counts, rest = [largest] + [least] * (amount - 1), total - largest - least * (amount - 1)
    while rest > 0:
        movable = [i for i in range(1, amount) if counts[i] < largest] or [i for i in range(1, amount) if counts[i] < bound]
        mass, budget = sum([loads[i] for i in movable]), rest
        for i in movable:
            extra = min(bound - counts[i], max(1, budget * loads[i] // mass), rest)
            counts[i] = counts[i] + extra
            rest = rest - extra
    return np.array(counts)


def noise(rng, extent, scale, reach, split=(), kind=jnp.bfloat16):
    values = scale * jax.random.normal(rng, extent, jnp.float32)
    if split:
        values = values * levels(rng, extent, split, -0.22, 0.18)
    return jnp.clip(values, -reach, reach).astype(kind)


def setup_inputs(seed: int = 0) -> dict:
    keys = jax.random.split(jax.random.key(seed), 12)
    harmonic_state = noise(keys[0], (NT, NE * DOF), 1.0, 6.0, ((0, 32), (1, 8)))
    direction = noise(keys[1], (NT, NE * DOF), 1.0, 6.0, ((0, 32), (1, 8)))
    source = noise(keys[2], (NT, NE * DOF), 1.0, 6.0, ((0, 32), (1, 8)), jnp.float32)
    jacobian = noise(keys[3], (NT, NE, DOF * DOF), DOF ** -0.5, 0.3125, ((0, 32), (1, 8)))
    frequency = jnp.clip(jnp.exp(jax.random.uniform(keys[4], (1,), jnp.float32, math.log(0.05), math.log(0.2))), 0.05, 0.2)
    viscosity = jnp.clip(jnp.exp(jax.random.uniform(keys[5], (1,), jnp.float32, math.log(0.01), math.log(0.03))), 0.01, 0.03)
    quad_weight = jnp.clip(jnp.exp(jax.random.uniform(keys[6], (NQ,), jnp.float32, math.log(0.3), math.log(3.0))), 0.3, 3.0)
    partner_device_keys = jax.random.split(jax.random.fold_in(keys[7], 1), NT * SLOTS // OVL)
    partner_device_turns = jax.random.permutation(jax.random.fold_in(keys[7], 3), NT * SLOTS // OVL)
    partner_device = jax.vmap(lambda own, number: deal_out(jax.random.fold_in(keys[7], 2), own, number, OVL, N_SPACE, 1, CAP, 2))(partner_device_keys, partner_device_turns).reshape((NT, SLOTS, 1))
    partner_face = set_ends(jax.random.randint(keys[8], (NT, SLOTS), 0, FACES_DEV), jax.random.fold_in(keys[8], 1), 0, FACES_DEV - 1).astype(jnp.int32)
    local_face = set_ends(jax.random.randint(keys[9], (NT, SLOTS), 0, FACES_DEV), jax.random.fold_in(keys[9], 1), 0, FACES_DEV - 1).astype(jnp.int32)
    weight_index = set_ends(jax.random.randint(keys[10], (NT, SLOTS), 0, NQ), jax.random.fold_in(keys[10], 1), 0, NQ - 1).astype(jnp.int32)
    return {"harmonic_state": harmonic_state, "direction": direction, "source": source, "jacobian": jacobian, "frequency": frequency, "viscosity": viscosity, "quad_weight": quad_weight, "partner_device": partner_device, "partner_face": partner_face, "local_face": local_face, "weight_index": weight_index}


def spectral_matrix(frequency, viscosity, length):
    indices = jnp.arange(length, dtype=jnp.int32)
    offsets = indices[:, None] - indices[None, :]
    on_diag = offsets == 0
    angles = jnp.where(on_diag, 0.5 * jnp.pi, jnp.pi * offsets.astype(jnp.float32) / length)
    parity = 1.0 - 2.0 * (jnp.abs(offsets) % 2).astype(jnp.float32)
    sine_values = jnp.sin(angles)
    first_order = jnp.where(on_diag, 0.0, 0.5 * parity * jnp.cos(angles) / sine_values)
    second = jnp.where(on_diag, -(length * length + 2) / 12.0, -parity / (2.0 * sine_values * sine_values))
    return frequency[0] * first_order + viscosity[0] * second


def face_table(fields_stack):
    last_node = fields_stack.shape[-1] - 1
    pieces_list = [fields_stack[:, :, :, 0], fields_stack[:, :, :, last_node],
                   fields_stack[:, :, :, :, 0], fields_stack[:, :, :, :, last_node],
                   fields_stack[:, :, :, :, :, 0], fields_stack[:, :, :, :, :, last_node]]
    stacked_faces = jnp.stack(pieces_list, axis=1)
    return stacked_faces.reshape(fields_stack.shape[0] * 6, -1)


def lift_faces(face_flux, template):
    last_node = template.shape[-1] - 1
    blocks = face_flux.reshape((template.shape[0], 6) + template.shape[1:-1])
    lifted = jnp.zeros(template.shape, jnp.float32)
    lifted = lifted.at[:, :, :, 0].add(blocks[:, 0])
    lifted = lifted.at[:, :, :, last_node].add(blocks[:, 1])
    lifted = lifted.at[:, :, :, :, 0].add(blocks[:, 2])
    lifted = lifted.at[:, :, :, :, last_node].add(blocks[:, 3])
    lifted = lifted.at[:, :, :, :, :, 0].add(blocks[:, 4])
    lifted = lifted.at[:, :, :, :, :, last_node].add(blocks[:, 5])
    return lifted


def slot_weights(quad_weight, weight_index):
    classes = jnp.arange(quad_weight.shape[0], dtype=jnp.int32)
    return jnp.sum(jnp.where(weight_index[:, None] == classes[None, :], quad_weight[None, :], 0.0), axis=1)


def reference(harmonic_state, direction, source, jacobian, frequency, viscosity, quad_weight, partner_device, partner_face, local_face, weight_index):
    spectral = spectral_matrix(frequency, viscosity, NT)
    time_state = jnp.dot(spectral, harmonic_state.astype(jnp.float32), precision=lax.Precision.HIGHEST)
    time_direction = jnp.dot(spectral, direction.astype(jnp.float32), precision=lax.Precision.HIGHEST)

    def one_instance(instance_inputs):
        state_row, direction_row, blocks, devices, far_faces, near_faces, classes = instance_inputs
        fields_stack = jnp.stack([state_row.reshape(NE, VARS, PNODE, PNODE, PNODE),
                                  direction_row.reshape(NE, VARS, PNODE, PNODE, PNODE)], axis=1)
        matrices = blocks.reshape(NE, DOF, DOF).astype(jnp.float32)
        flat_fields = fields_stack.reshape(NE, 2, DOF).astype(jnp.float32)
        element_terms = jnp.einsum("eab,ekb->eka", matrices, flat_fields, precision=lax.Precision.HIGHEST)
        trace_table = face_table(fields_stack).astype(jnp.float32)
        owners = jnp.arange(SLOTS, dtype=jnp.int32) // OVL
        near_ids = owners * FACES_DEV + near_faces
        far_ids = devices[:, 0] * FACES_DEV + far_faces
        weights = slot_weights(quad_weight, classes)
        slot_terms = weights[:, None] * (trace_table[near_ids] - trace_table[far_ids])
        face_flux = jax.ops.segment_sum(slot_terms, near_ids, num_segments=NE * 6)
        lifted = lift_faces(face_flux, fields_stack).reshape(NE, 2, DOF)
        summed = element_terms + lifted
        return summed[:, 0].reshape(-1), summed[:, 1].reshape(-1)

    local_state, local_direction = lax.map(one_instance, (harmonic_state, direction, jacobian, partner_device, partner_face, local_face, weight_index))
    residual = source - (time_state + local_state)
    product = time_direction + local_direction
    return residual, product
```

```python
import jax
import jax.numpy as jnp
import numpy as np
from jax import lax
from jax.experimental import pallas as pl
from jax.experimental.pallas import tpu as pltpu
from jax.sharding import PartitionSpec as P

VARS = 5
PNODE = 4
E_DEV = 48
DOF = 320
SLOTS_DEV = 192
N_SPACE = 8
NT = 32
FLAT = E_DEV * DOF
ROWS = FLAT // 128
CHUNKS = 10
GROUPS = 8
PIECE = GROUPS * 4 * DOF
GROUP = 8
TURNS = NT // GROUP
MIB = 1024 * 1024
F32 = jnp.float32
BF16 = jnp.bfloat16


def face_selector():
    table = np.zeros((DOF, 6 * 128), np.float32)
    for face in range(6):
        fixed = 0 if face % 2 == 0 else PNODE - 1
        for comp in range(VARS):
            for first in range(PNODE):
                for second in range(PNODE):
                    if face < 2:
                        i, j, k = fixed, first, second
                    elif face < 4:
                        i, j, k = first, fixed, second
                    else:
                        i, j, k = first, second, fixed
                    table[comp * 64 + i * 16 + j * 4 + k, face * 128 + comp * 16 + first * 4 + second] = 1.0
    return table


def face_incidence():
    rows = np.zeros((8, 384), np.float32)
    for face in range(6):
        rows[face, :DOF] = face_selector()[:, face * 128 : (face + 1) * 128].sum(axis=1)
    return rows


def lane_half(rows):
    return lax.broadcasted_iota(jnp.int32, (rows, 128), 1) < 64


def swap(x):
    return pltpu.roll(x, 64, 1)


def join(low, high):
    return jnp.where(lane_half(low.shape[0]), swap(low), swap(high))


def prep_kernel(s_ref, d_ref, copies_ref, elem_ref, flat, wide):
    for k, ref in enumerate((s_ref, d_ref)):
        for r in range(ROWS):
            flat[k * ROWS + r : k * ROWS + r + 1, :] = ref[0:1, r * 128 : (r + 1) * 128].astype(F32)
    half = E_DEV // 2
    low = lane_half(half)
    s = [flat[pl.ds(q, half, stride=5), :] for q in range(5)]
    d = [flat[pl.ds(ROWS + q, half, stride=5), :] for q in range(5)]
    even = [s[0], s[1], jnp.where(low, s[2], swap(d[0])), join(d[0], d[1]), join(d[1], d[2])]
    odd = [join(s[2], s[3]), join(s[3], s[4]), jnp.where(low, swap(s[4]), d[2]), d[3], d[4]]
    for q in range(5):
        wide[q, pl.ds(0, half, stride=2), :] = even[q]
        wide[q, pl.ds(1, half, stride=2), :] = odd[q]
    for q in range(5):
        tile = wide[q].astype(BF16)
        elem_ref[:, q * 128 : (q + 1) * 128] = tile
        for to in range(GROUP):
            copies_ref[to, :, q * 128 : (q + 1) * 128] = tile


def prep(state, direction):
    return pl.pallas_call(
        prep_kernel,
        out_shape=(
            jax.ShapeDtypeStruct((GROUP, E_DEV, 2 * DOF), BF16),
            jax.ShapeDtypeStruct((E_DEV, 2 * DOF), BF16),
        ),
        in_specs=[pl.BlockSpec(memory_space=pltpu.VMEM)] * 2,
        out_specs=(pl.BlockSpec(memory_space=pltpu.VMEM),) * 2,
        scratch_shapes=[pltpu.VMEM((2 * ROWS, 128), F32), pltpu.VMEM((5, E_DEV, 128), F32)],
        compiler_params=pltpu.CompilerParams(vmem_limit_bytes=4 * MIB),
        name="prep",
    )(state, direction)


def circulant_parts():
    j = np.arange(1, NT)
    sign = 1.0 - 2.0 * (j % 2)
    angle = np.pi * j / NT
    first = np.concatenate([[0.0], 0.5 * sign * np.cos(angle) / np.sin(angle)])
    second = np.concatenate([[-(NT * NT + 2) / 12.0], -sign / (2.0 * np.sin(angle) ** 2)])
    return first, second


def partial_kernel(place_ref, table_ref, freq_ref, visc_ref, x_ref, y_ref):
    place = place_ref[0]
    row, col = place // GROUP, place % GROUP
    freq, visc = freq_ref[0], visc_ref[0]
    coef = []
    for y in range(TURNS):
        for a in range(GROUP):
            j = ((y - row) * GROUP + col - a) & (NT - 1)
            coef.append(jnp.full((8, 128), freq * table_ref[0, j] + visc * table_ref[1, j], F32))
    for r in range(E_DEV // 16):
        for q in range(5):
            x = [
                x_ref[a, r * 16 : (r + 1) * 16, q * 128 : (q + 1) * 128].astype(F32)
                for a in range(GROUP)
            ]
            for h in range(2):
                part = [v[h * 8 : (h + 1) * 8] for v in x]
                for y in range(TURNS):
                    acc = coef[y * GROUP] * part[0]
                    for a in range(1, GROUP):
                        acc = acc + coef[y * GROUP + a] * part[a]
                    y_ref[y, r * 16 + h * 8 : r * 16 + (h + 1) * 8, q * 128 : (q + 1) * 128] = acc


def partial_sums(place, frequency, viscosity, gathered):
    smem = pl.BlockSpec(memory_space=pltpu.SMEM)
    vmem = pl.BlockSpec(memory_space=pltpu.VMEM)
    table = jnp.asarray(np.stack(circulant_parts()), F32)
    return pl.pallas_call(
        partial_kernel,
        out_shape=jax.ShapeDtypeStruct((TURNS, E_DEV, 2 * DOF), F32),
        in_specs=[smem, smem, smem, smem, vmem],
        out_specs=vmem,
        compiler_params=pltpu.CompilerParams(vmem_limit_bytes=4 * MIB),
        name="partial_sums",
    )(place, table, frequency, viscosity, gathered)


def vector_tiles(elem):
    p = [elem[:, q * 128 : (q + 1) * 128] for q in range(5)]
    low = lane_half(E_DEV)
    zero = jnp.zeros((E_DEV, 128), F32)
    s = [p[0], p[1], jnp.where(low, p[2], zero), jnp.where(low, zero, swap(p[0])), join(p[0], p[1]), join(p[1], p[2])]
    d = [join(p[2], p[3]), join(p[3], p[4]), jnp.where(low, swap(p[4]), zero), jnp.where(low, zero, p[2]), p[3], p[4]]
    return s, d


def jacobian_kernel(jac_ref, elem_ref, out_ref, held, weights, acc, rows, sems):
    copies = [
        pltpu.make_async_copy(jac_ref.at[0, :, pl.ds(c * PIECE, PIECE)], held.at[c], sems.at[c])
        for c in range(CHUNKS)
    ]
    for copy in copies:
        copy.start()
    s, d = vector_tiles(elem_ref[...].astype(F32))
    pad = jnp.zeros((128 - 2 * E_DEV, 128), F32)
    x0, x1, x2, y0, y1, y2 = [
        jnp.concatenate([a, b, pad], axis=0).T.astype(BF16) for a, b in zip(s, d)
    ]
    zero = jnp.zeros((128, 128), BF16)
    layout = (
        ((x0, zero), (x1, zero)),
        ((x2, y0), (zero, y1)),
        ((y2, zero), (zero, x0)),
        ((x1, zero), (x2, y0)),
        ((y1, zero), (y2, zero)),
    )
    for t in range(5):
        for i in range(2):
            for j in range(2):
                weights[t, i * 128 : (i + 1) * 128, j * 128 : (j + 1) * 128] = layout[t][i][j]
    e = lax.broadcasted_iota(jnp.int32, (E_DEV, 128), 0)
    lane = lax.broadcasted_iota(jnp.int32, (E_DEV, 128), 1)
    keep = (lane == e) | (lane == e + E_DEV)

    def step(c, carry):
        start = pl.multiple_of(c * PIECE, PIECE)
        pltpu.make_async_copy(jac_ref.at[0, :, pl.ds(start, PIECE)], held.at[c], sems.at[c]).wait()
        res = []
        for t in range(5):
            lhs = jnp.concatenate(
                [held[c, :, (g * 5 + t) * 256 : (g * 5 + t + 1) * 256] for g in range(GROUPS)], axis=0
            )
            w = weights[t] if t in (1, 2, 3) else weights[t][:, :128]
            res.append(jnp.dot(lhs, w, preferred_element_type=F32))
        pairs = (
            res[0] + res[1][:, :128],
            res[1][:, 128:] + res[2][:, :128],
            res[2][:, 128:] + res[3][:, :128],
            res[3][:, 128:] + res[4],
        )
        for i in range(4):
            r = jnp.where(keep[None], pairs[i].reshape(GROUPS, E_DEV, 128), 0.0)
            acc[i, pl.ds(pl.multiple_of(c * GROUPS, GROUPS), GROUPS), :] = jnp.sum(r, axis=1)
        return carry

    lax.fori_loop(0, CHUNKS, step, 0)
    for i in range(4):
        rows[pl.ds(i, CHUNKS * GROUPS, stride=4), :] = acc[i]
    rows[DOF:, :] = jnp.zeros((384 - DOF, 128), F32)
    for q in range(3):
        out_ref[:, q * 128 : (q + 1) * 128] = rows[q * 128 : (q + 1) * 128, :].T


def jacobian_product(jacobian, elem):
    return pl.pallas_call(
        jacobian_kernel,
        out_shape=jax.ShapeDtypeStruct((128, 384), F32),
        in_specs=[pl.BlockSpec(memory_space=pl.ANY), pl.BlockSpec(memory_space=pltpu.VMEM)],
        out_specs=pl.BlockSpec(memory_space=pltpu.VMEM),
        scratch_shapes=[
            pltpu.VMEM((CHUNKS, E_DEV, PIECE), BF16),
            pltpu.VMEM((5, 256, 256), BF16),
            pltpu.VMEM((4, CHUNKS * GROUPS, 128), F32),
            pltpu.VMEM((384, 128), F32),
            pltpu.SemaphoreType.DMA((CHUNKS,)),
        ],
        compiler_params=pltpu.CompilerParams(vmem_limit_bytes=49 * MIB),
        cost_estimate=pl.CostEstimate(
            flops=2 * 2 * E_DEV * DOF * DOF * 48, bytes_accessed=2 * E_DEV * DOF * DOF, transcendentals=0
        ),
        name="jacobian",
    )(jacobian, elem)


def split(x):
    high = x.astype(BF16)
    return high, (x - high.astype(F32)).astype(BF16)


def flux_kernel(quad_ref, dev_ref, far_ref, near_ref, cls_ref, elem_ref, jac_ref, sel_ref, inc_ref, table_ref, out_ref):
    far = far_ref[...]
    near = near_ref[...]
    cls = cls_ref[...]
    far_e = (far * 10923) >> 16
    far_l = far - far_e * 6
    near_e = (near * 10923) >> 16
    near_row = (near - near_e * 6) * E_DEV + near_e
    column = dev_ref[...] * E_DEV + far_e
    w = jnp.zeros((1, SLOTS_DEV), F32)
    for c in range(16):
        w = jnp.where(cls == c, quad_ref[c], w)
    r = lax.broadcasted_iota(jnp.int32, (SLOTS_DEV, SLOTS_DEV), 0)
    c = lax.broadcasted_iota(jnp.int32, (SLOTS_DEV, SLOTS_DEV), 1)
    both = (far_l * 512 + column).astype(F32)
    code = jnp.sum(jnp.where(r == c, both, 0.0), axis=1, keepdims=True).astype(jnp.int32)
    column_s = code & 511
    far_ls = code >> 9
    total = N_SPACE * E_DEV
    pick = (lax.broadcasted_iota(jnp.int32, (SLOTS_DEV, total), 1) == column_s).astype(F32).astype(BF16)
    table = table_ref[...].reshape(total, 2 * DOF)
    got = jnp.dot(pick, table, preferred_element_type=F32)
    p = [got[:, q * 128 : (q + 1) * 128] for q in range(5)]
    low = lane_half(SLOTS_DEV)
    zero = jnp.zeros((SLOTS_DEV, 128), F32)
    fields = jnp.concatenate(
        [
            jnp.concatenate([p[0], p[1], jnp.where(low, p[2], zero)], axis=1),
            jnp.concatenate([join(p[2], p[3]), join(p[3], p[4]), jnp.where(low, swap(p[4]), zero)], axis=1),
        ],
        axis=0,
    ).astype(BF16)
    sel = sel_ref[...]
    faces = jnp.dot(fields, sel, preferred_element_type=F32)
    which = jnp.concatenate([far_ls, far_ls], axis=0)
    trace = jnp.zeros((2 * SLOTS_DEV, 128), F32)
    for face in range(6):
        trace = jnp.where(which == face, faces[:, face * 128 : (face + 1) * 128], trace)
    trace = jnp.concatenate([trace[:SLOTS_DEV], trace[SLOTS_DEV:]], axis=1).astype(BF16)
    rows = lax.broadcasted_iota(jnp.int32, (6 * E_DEV, SLOTS_DEV), 0)
    spread = jnp.where(rows == near_row, w, 0.0)
    high, rest_w = split(spread)
    flux = jnp.dot(high, trace, preferred_element_type=F32) + jnp.dot(rest_w, trace, preferred_element_type=F32)
    weight_sum = jnp.sum(spread, axis=1, keepdims=True)
    lhs = jnp.concatenate(
        [
            jnp.concatenate(
                [flux[f * E_DEV : (f + 1) * E_DEV, :128], flux[f * E_DEV : (f + 1) * E_DEV, 128:]], axis=0
            )
            for f in range(6)
        ],
        axis=1,
    )
    high, rest_f = split(lhs)
    dims = (((1,), (1,)), ((), ()))
    lifted = lax.dot_general(high, sel, dims, preferred_element_type=F32) + lax.dot_general(
        rest_f, sel, dims, preferred_element_type=F32
    )
    coef = jnp.zeros((E_DEV, 384), F32)
    for f in range(6):
        coef = coef + weight_sum[f * E_DEV : (f + 1) * E_DEV] * inc_ref[f : f + 1, :]
    fields_own = vector_tiles(elem_ref[...].astype(F32))
    for k in range(2):
        own = jnp.concatenate(fields_own[k][:3], axis=1)
        rows_k = slice(k * E_DEV, (k + 1) * E_DEV)
        out_ref[rows_k, :] = jac_ref[rows_k, :] + coef * own - lifted[rows_k]


def space_terms(quad, dev, far, near, cls, elem, jac_terms, table):
    sel = np.zeros((384, 768), np.float32)
    sel[:DOF] = face_selector()
    vmem = pl.BlockSpec(memory_space=pltpu.VMEM)
    return pl.pallas_call(
        flux_kernel,
        out_shape=jax.ShapeDtypeStruct((2 * E_DEV, 384), F32),
        in_specs=[pl.BlockSpec(memory_space=pltpu.SMEM)] + [vmem] * 9,
        out_specs=vmem,
        compiler_params=pltpu.CompilerParams(vmem_limit_bytes=12 * MIB),
        name="space_terms",
    )(
        quad, dev, far, near, cls, elem, jac_terms,
        jnp.asarray(sel, BF16), jnp.asarray(face_incidence()), table,
    )


def final_kernel(src_ref, time_ref, space_ref, res_ref, prod_ref, scratch):
    total = time_ref[0]
    for y in range(1, TURNS):
        total = total + time_ref[y]
    times = vector_tiles(total)
    half = E_DEV // 2
    low = lane_half(half)
    for k, out_ref in enumerate((res_ref, prod_ref)):
        for q in range(3):
            scratch[q] = space_ref[k * E_DEV : (k + 1) * E_DEV, q * 128 : (q + 1) * 128] + times[k][q]
        even = [scratch[q, pl.ds(0, half, stride=2), :] for q in range(3)]
        odd = [scratch[q, pl.ds(1, half, stride=2), :] for q in range(3)]
        tiles = [
            even[0],
            even[1],
            jnp.where(low, even[2], swap(odd[0])),
            join(odd[0], odd[1]),
            join(odd[1], odd[2]),
        ]
        for q in range(5):
            at = tiles[q]
            if k == 0:
                at = src_ref[pl.ds(q, half, stride=5), :] - at
            out_ref[pl.ds(q, half, stride=5), :] = at


def finish(source, time_parts, space):
    vmem = pl.BlockSpec(memory_space=pltpu.VMEM)
    return pl.pallas_call(
        final_kernel,
        out_shape=(jax.ShapeDtypeStruct((ROWS, 128), F32),) * 2,
        in_specs=[vmem] * 3,
        out_specs=(vmem, vmem),
        scratch_shapes=[pltpu.VMEM((3, E_DEV, 128), F32)],
        compiler_params=pltpu.CompilerParams(vmem_limit_bytes=4 * MIB),
        name="finish",
    )(source, time_parts, space)


def per_device(
    harmonic_state,
    direction,
    source,
    jacobian,
    frequency,
    viscosity,
    quad_weight,
    partner_device,
    partner_face,
    local_face,
    weight_index,
):
    copies, elem = prep(harmonic_state, direction)
    place = lax.axis_index("inst").reshape(1)
    table = lax.all_to_all(copies, "space", 0, 0, tiled=True)
    rows = [[y * GROUP + a for a in range(GROUP)] for y in range(TURNS)]
    columns = [[y * GROUP + a for y in range(TURNS)] for a in range(GROUP)]
    gathered = lax.all_to_all(copies, "inst", 0, 0, axis_index_groups=rows, tiled=True)
    parts = partial_sums(place, frequency, viscosity, gathered)
    time_parts = lax.all_to_all(parts, "inst", 0, 0, axis_index_groups=columns, tiled=True)
    jac_terms = jacobian_product(jacobian, elem)
    space = space_terms(
        quad_weight,
        partner_device.reshape(1, SLOTS_DEV),
        partner_face,
        local_face,
        weight_index,
        elem,
        jac_terms,
        table,
    )
    residual, product = finish(source.reshape(ROWS, 128), time_parts, space)
    return residual.reshape(1, FLAT), product.reshape(1, FLAT)


def solution(mesh):
    in_specs = (
        P("inst", "space"),
        P("inst", "space"),
        P("inst", "space"),
        P("inst", "space", None),
        P(),
        P(),
        P(),
        P("inst", "space", None),
        P("inst", "space"),
        P("inst", "space"),
        P("inst", "space"),
    )
    out_specs = (P("inst", "space"), P("inst", "space"))
    return jax.shard_map(
        per_device, mesh=mesh, in_specs=in_specs, out_specs=out_specs, check_vma=False
    )
```

```python
import jax
import jax.numpy as jnp
import numpy as np
from jax import lax
from jax.experimental import pallas as pl
from jax.experimental.pallas import tpu as pltpu
from jax.sharding import PartitionSpec as P

VARS = 5
PNODE = 4
E_DEV = 48
DOF = 320
SLOTS_DEV = 192
N_SPACE = 8
NT = 32
FLAT = E_DEV * DOF
ROWS = FLAT // 128
CHUNKS = 5
GROUPS = 16
BLOCK = 16
PIECE = GROUPS * 4 * DOF
MIB = 1024 * 1024
F32 = jnp.float32
BF16 = jnp.bfloat16


def face_selector():
    table = np.zeros((DOF, 6 * 128), np.float32)
    for face in range(6):
        fixed = 0 if face % 2 == 0 else PNODE - 1
        for comp in range(VARS):
            for first in range(PNODE):
                for second in range(PNODE):
                    if face < 2:
                        i, j, k = fixed, first, second
                    elif face < 4:
                        i, j, k = first, fixed, second
                    else:
                        i, j, k = first, second, fixed
                    table[comp * 64 + i * 16 + j * 4 + k, face * 128 + comp * 16 + first * 4 + second] = 1.0
    return table


def face_incidence():
    rows = np.zeros((8, 384), np.float32)
    for face in range(6):
        rows[face, :DOF] = face_selector()[:, face * 128 : (face + 1) * 128].sum(axis=1)
    return rows


def lane_half(rows):
    return lax.broadcasted_iota(jnp.int32, (rows, 128), 1) < 64


def swap(x):
    return pltpu.roll(x, 64, 1)


def join(low, high):
    return jnp.where(lane_half(low.shape[0]), swap(low), swap(high))


def prep_kernel(s_hbm, d_hbm, send_ref, elem_ref, held, flat, wide, sems):
    copies = [pltpu.make_async_copy(ref, held.at[k], sems.at[k]) for k, ref in enumerate((s_hbm, d_hbm))]
    for copy in copies:
        copy.start()
    for k in range(2):
        copies[k].wait()
        for r in range(ROWS):
            flat[k * ROWS + r : k * ROWS + r + 1, :] = held[k, 0:1, r * 128 : (r + 1) * 128].astype(F32)
    flat[2 * ROWS : 256, :] = jnp.zeros((256 - 2 * ROWS, 128), F32)
    send_ref[...] = flat[...].astype(BF16)
    half = E_DEV // 2
    low = lane_half(half)
    s = [flat[pl.ds(q, half, stride=5), :] for q in range(5)]
    d = [flat[pl.ds(ROWS + q, half, stride=5), :] for q in range(5)]
    even = [s[0], s[1], jnp.where(low, s[2], swap(d[0])), join(d[0], d[1]), join(d[1], d[2])]
    odd = [join(s[2], s[3]), join(s[3], s[4]), jnp.where(low, swap(s[4]), d[2]), d[3], d[4]]
    for q in range(5):
        wide[q, pl.ds(0, half, stride=2), :] = even[q]
        wide[q, pl.ds(1, half, stride=2), :] = odd[q]
    for q in range(5):
        elem_ref[:, q * 128 : (q + 1) * 128] = wide[q].astype(BF16)


def prep(state, direction):
    return pl.pallas_call(
        prep_kernel,
        out_shape=(
            jax.ShapeDtypeStruct((256, 128), BF16),
            jax.ShapeDtypeStruct((E_DEV, 2 * DOF), BF16),
        ),
        in_specs=[pl.BlockSpec(memory_space=pltpu.HBM)] * 2,
        out_specs=(pl.BlockSpec(memory_space=pltpu.VMEM),) * 2,
        scratch_shapes=[
            pltpu.VMEM((2, 1, FLAT), BF16),
            pltpu.VMEM((256, 128), F32),
            pltpu.VMEM((5, E_DEV, 128), F32),
            pltpu.SemaphoreType.DMA((2,)),
        ],
        compiler_params=pltpu.CompilerParams(vmem_limit_bytes=4 * MIB),
        name="prep",
    )(state, direction)


def circulant_parts():
    j = np.arange(1, NT)
    sign = 1.0 - 2.0 * (j % 2)
    angle = np.pi * j / NT
    first = np.concatenate([[0.0], 0.5 * sign * np.cos(angle) / np.sin(angle)])
    second = np.concatenate([[-(NT * NT + 2) / 12.0], -sign / (2.0 * np.sin(angle) ** 2)])
    return first, second


def spectral_kernel(freq_ref, visc_ref, x_ref, own_ref, left_ref, right_ref, far_ref, y_ref, to_right_ref, to_left_ref):
    to_right_ref[:E_DEV, :] = own_ref[...]
    to_right_ref[E_DEV:, :] = left_ref[...]
    to_left_ref[:E_DEV, :] = own_ref[...]
    to_left_ref[E_DEV:, :] = right_ref[...]
    first, second = circulant_parts()
    freq, visc = freq_ref[0], visc_ref[0]
    half = NT // 2
    x = x_ref[...].astype(F32).reshape(NT, 8, 128)

    def coef(a, b):
        return jnp.full((8, 128), freq * float(a) + visc * float(b), F32)

    def part(sgn):
        c = [
            coef(0.5 * (first[j] + sgn * first[j + half]), 0.5 * (second[j] + sgn * second[j + half]))
            for j in range(half)
        ]
        u = [x[s] + sgn * x[s + half] for s in range(half)]
        out = []
        for t in range(half):
            acc = None
            for s in range(half):
                j = t - s
                term = c[j % half] * u[s]
                if acc is None:
                    acc = term
                elif j < 0 and sgn < 0:
                    acc = acc - term
                else:
                    acc = acc + term
            out.append(acc)
        return out

    even = part(1.0)
    for t in range(half):
        y_ref[t * 8 : (t + 1) * 8, :] = even[t]
    odd = part(-1.0)
    for t in range(half):
        e = y_ref[t * 8 : (t + 1) * 8, :]
        y_ref[t * 8 : (t + 1) * 8, :] = e + odd[t]
        y_ref[(t + half) * 8 : (t + half + 1) * 8, :] = e - odd[t]


def spectral_sum(frequency, viscosity, received, own, left, right, far):
    smem = pl.BlockSpec(memory_space=pltpu.SMEM)
    vmem = pl.BlockSpec(memory_space=pltpu.VMEM)
    pair = jax.ShapeDtypeStruct((2 * E_DEV, 2 * DOF), BF16)
    return pl.pallas_call(
        spectral_kernel,
        out_shape=(jax.ShapeDtypeStruct((256, 128), F32), pair, pair),
        in_specs=[smem, smem] + [vmem] * 4 + [pl.BlockSpec(memory_space=pl.ANY)],
        out_specs=(vmem,) * 3,
        compiler_params=pltpu.CompilerParams(vmem_limit_bytes=4 * MIB),
        name="spectral",
    )(frequency, viscosity, received, own, left, right, far)


def vector_tiles(elem):
    p = [elem[:, q * 128 : (q + 1) * 128] for q in range(5)]
    low = lane_half(E_DEV)
    zero = jnp.zeros((E_DEV, 128), F32)
    s = [p[0], p[1], jnp.where(low, p[2], zero), jnp.where(low, zero, swap(p[0])), join(p[0], p[1]), join(p[1], p[2])]
    d = [join(p[2], p[3]), join(p[3], p[4]), jnp.where(low, swap(p[4]), zero), jnp.where(low, zero, p[2]), p[3], p[4]]
    return s, d


def jacobian_kernel(jac_hbm, elem_ref, after_ref, out_ref, held, weights, acc, rows, sems):
    def piece(c, start):
        return pltpu.make_async_copy(jac_hbm.at[0, :, pl.ds(start, PIECE)], held.at[c], sems.at[c])

    for c in range(CHUNKS):
        piece(c, c * PIECE).start()
    s, d = vector_tiles(elem_ref[...].astype(F32))
    pad = jnp.zeros((128 - 2 * E_DEV, 128), F32)
    blocks = E_DEV // BLOCK
    turned = []
    for q in range(3):
        parts = []
        for b in range(blocks):
            parts += [s[q][b * BLOCK : (b + 1) * BLOCK], d[q][b * BLOCK : (b + 1) * BLOCK]]
        turned.append(jnp.concatenate(parts + [pad], axis=0).T)
    turned = jnp.concatenate(turned, axis=0)[:DOF]
    lane = lax.broadcasted_iota(jnp.int32, (DOF, 128), 1)
    for b in range(blocks):
        for i in range(4):
            at = turned if i == b else pltpu.roll(turned, (i - b) * 32 % 128, 1)
            at = jnp.where((lane >= 32 * i) & (lane < 32 * (i + 1)), at, 0.0)
            weights[b, DOF * i : DOF * (i + 1), :] = at.astype(BF16)
    e = lax.broadcasted_iota(jnp.int32, (BLOCK, 128), 0)
    keep = (lax.broadcasted_iota(jnp.int32, (BLOCK, 128), 1) & (BLOCK - 1)) == e

    def step(c, carry):
        piece(c, pl.multiple_of(c * PIECE, PIECE)).wait()
        for b in range(blocks):
            lhs = jnp.concatenate(
                [
                    held[c, b * BLOCK : (b + 1) * BLOCK, g * 4 * DOF : (g + 1) * 4 * DOF]
                    for g in range(GROUPS)
                ],
                axis=0,
            )
            res = jnp.dot(lhs, weights[b], preferred_element_type=F32)
            res = jnp.where(keep[None], res.reshape(GROUPS, BLOCK, 128), 0.0)
            acc[b, pl.ds(pl.multiple_of(c * GROUPS, GROUPS), GROUPS), :] = jnp.sum(res, axis=1)
        return carry

    lax.fori_loop(0, CHUNKS, step, 0)
    groups = CHUNKS * GROUPS
    lane = lax.broadcasted_iota(jnp.int32, (groups, 128), 1)
    for i in range(4):
        at = jnp.zeros((groups, 128), F32)
        for b in range(blocks):
            moved = acc[b] if i == b else pltpu.roll(acc[b], (b - i) * 32 % 128, 1)
            at = jnp.where((lane >= 32 * b) & (lane < 32 * (b + 1)), moved, at)
        rows[pl.ds(i, groups, stride=4), :] = at
    rows[DOF:, :] = jnp.zeros((384 - DOF, 128), F32)
    for q in range(3):
        back = rows[q * 128 : (q + 1) * 128, :].T
        for b in range(blocks):
            for k in range(2):
                out_ref[k * E_DEV + b * BLOCK : k * E_DEV + (b + 1) * BLOCK, q * 128 : (q + 1) * 128] = back[
                    b * 32 + k * BLOCK : b * 32 + (k + 1) * BLOCK
                ]


def jacobian_product(jacobian, elem, after):
    return pl.pallas_call(
        jacobian_kernel,
        out_shape=jax.ShapeDtypeStruct((2 * E_DEV, 384), F32),
        in_specs=[
            pl.BlockSpec(memory_space=pltpu.HBM),
            pl.BlockSpec(memory_space=pltpu.VMEM),
            pl.BlockSpec(memory_space=pl.ANY),
        ],
        out_specs=pl.BlockSpec(memory_space=pltpu.VMEM),
        scratch_shapes=[
            pltpu.VMEM((CHUNKS, E_DEV, PIECE), BF16),
            pltpu.VMEM((E_DEV // BLOCK, 4 * DOF, 128), BF16),
            pltpu.VMEM((E_DEV // BLOCK, CHUNKS * GROUPS, 128), F32),
            pltpu.VMEM((384, 128), F32),
            pltpu.SemaphoreType.DMA((CHUNKS,)),
        ],
        compiler_params=pltpu.CompilerParams(vmem_limit_bytes=49 * MIB),
        cost_estimate=pl.CostEstimate(
            flops=2 * 2 * E_DEV * DOF * DOF * 48, bytes_accessed=2 * E_DEV * DOF * DOF, transcendentals=0
        ),
        name="jacobian",
    )(jacobian, elem, after)


def split(x):
    high = x.astype(BF16)
    return high, (x - high.astype(F32)).astype(BF16)


def flux_kernel(
    me_ref, quad_ref, dev_ref, far_ref, near_ref, cls_ref, jac_ref, sel_ref, inc_ref, elem_ref, *rest
):
    tables, out_ref = rest[:-1], rest[-1]
    me = me_ref[0]
    far = far_ref[...]
    near = near_ref[...]
    cls = cls_ref[...]
    far_e = (far * 10923) >> 16
    far_l = far - far_e * 6
    near_e = (near * 10923) >> 16
    near_row = (near - near_e * 6) * E_DEV + near_e
    turn = (dev_ref[...] - me) & (N_SPACE - 1)
    block = jnp.zeros((1, SLOTS_DEV), jnp.int32)
    for at, which in enumerate((0, 7, 1, 4, 6, 5, 2, 3)):
        block = jnp.where(turn == which, at, block)
    column = block * E_DEV + far_e
    w = jnp.zeros((1, SLOTS_DEV), F32)
    for c in range(16):
        w = jnp.where(cls == c, quad_ref[c], w)
    r = lax.broadcasted_iota(jnp.int32, (SLOTS_DEV, SLOTS_DEV), 0)
    c = lax.broadcasted_iota(jnp.int32, (SLOTS_DEV, SLOTS_DEV), 1)
    both = (far_l * 512 + column).astype(F32)
    code = jnp.sum(jnp.where(r == c, both, 0.0), axis=1, keepdims=True).astype(jnp.int32)
    column_s = code & 511
    far_ls = code >> 9
    total = N_SPACE * E_DEV
    pick = (lax.broadcasted_iota(jnp.int32, (SLOTS_DEV, total), 1) == column_s).astype(F32).astype(BF16)
    table = jnp.concatenate([elem_ref[...]] + [t[...] for t in tables], axis=0)
    got = jnp.dot(pick, table, preferred_element_type=F32)
    p = [got[:, q * 128 : (q + 1) * 128] for q in range(5)]
    low = lane_half(SLOTS_DEV)
    zero = jnp.zeros((SLOTS_DEV, 128), F32)
    fields = jnp.concatenate(
        [
            jnp.concatenate([p[0], p[1], jnp.where(low, p[2], zero)], axis=1),
            jnp.concatenate([join(p[2], p[3]), join(p[3], p[4]), jnp.where(low, swap(p[4]), zero)], axis=1),
        ],
        axis=0,
    ).astype(BF16)
    sel = sel_ref[...]
    faces = jnp.dot(fields, sel, preferred_element_type=F32)
    which = jnp.concatenate([far_ls, far_ls], axis=0)
    trace = jnp.zeros((2 * SLOTS_DEV, 128), F32)
    for face in range(6):
        trace = jnp.where(which == face, faces[:, face * 128 : (face + 1) * 128], trace)
    trace = jnp.concatenate([trace[:SLOTS_DEV], trace[SLOTS_DEV:]], axis=1).astype(BF16)
    rows = lax.broadcasted_iota(jnp.int32, (6 * E_DEV, SLOTS_DEV), 0)
    spread = jnp.where(rows == near_row, w, 0.0)
    high, rest_w = split(spread)
    flux = jnp.dot(high, trace, preferred_element_type=F32) + jnp.dot(rest_w, trace, preferred_element_type=F32)
    weight_sum = jnp.sum(spread, axis=1, keepdims=True)
    lhs = jnp.concatenate(
        [
            jnp.concatenate(
                [flux[f * E_DEV : (f + 1) * E_DEV, :128], flux[f * E_DEV : (f + 1) * E_DEV, 128:]], axis=0
            )
            for f in range(6)
        ],
        axis=1,
    )
    high, rest_f = split(lhs)
    dims = (((1,), (1,)), ((), ()))
    lifted = lax.dot_general(high, sel, dims, preferred_element_type=F32) + lax.dot_general(
        rest_f, sel, dims, preferred_element_type=F32
    )
    coef = jnp.zeros((E_DEV, 384), F32)
    for f in range(6):
        coef = coef + weight_sum[f * E_DEV : (f + 1) * E_DEV] * inc_ref[f : f + 1, :]
    fields_own = vector_tiles(elem_ref[...].astype(F32))
    for k in range(2):
        own = jnp.concatenate(fields_own[k][:3], axis=1)
        rows_k = slice(k * E_DEV, (k + 1) * E_DEV)
        out_ref[rows_k, :] = jac_ref[rows_k, :] + coef * own - lifted[rows_k]


def space_terms(me, quad, dev, far, near, cls, jac_terms, elem, tables):
    sel = np.zeros((384, 768), np.float32)
    sel[:DOF] = face_selector()
    vmem = pl.BlockSpec(memory_space=pltpu.VMEM)
    return pl.pallas_call(
        flux_kernel,
        out_shape=jax.ShapeDtypeStruct((2 * E_DEV, 384), F32),
        in_specs=[pl.BlockSpec(memory_space=pltpu.SMEM)] * 2 + [vmem] * (8 + len(tables)),
        out_specs=vmem,
        compiler_params=pltpu.CompilerParams(vmem_limit_bytes=12 * MIB),
        name="space_terms",
    )(
        me, quad, dev, far, near, cls, jac_terms,
        jnp.asarray(sel, BF16), jnp.asarray(face_incidence()), elem, *tables,
    )


def final_kernel(src_ref, time_ref, space_ref, res_ref, prod_ref, scratch):
    half = E_DEV // 2
    low = lane_half(half)
    for k, out_ref in enumerate((res_ref, prod_ref)):
        for q in range(3):
            scratch[q] = space_ref[k * E_DEV : (k + 1) * E_DEV, q * 128 : (q + 1) * 128]
        even = [scratch[q, pl.ds(0, half, stride=2), :] for q in range(3)]
        odd = [scratch[q, pl.ds(1, half, stride=2), :] for q in range(3)]
        tiles = [
            even[0],
            even[1],
            jnp.where(low, even[2], swap(odd[0])),
            join(odd[0], odd[1]),
            join(odd[1], odd[2]),
        ]
        for q in range(5):
            at = time_ref[pl.ds(k * ROWS + q, half, stride=5), :] + tiles[q]
            if k == 0:
                at = src_ref[pl.ds(q, half, stride=5), :] - at
            out_ref[pl.ds(q, half, stride=5), :] = at


def finish(source, time_parts, space):
    vmem = pl.BlockSpec(memory_space=pltpu.VMEM)
    return pl.pallas_call(
        final_kernel,
        out_shape=(jax.ShapeDtypeStruct((ROWS, 128), F32),) * 2,
        in_specs=[vmem] * 3,
        out_specs=(vmem, vmem),
        scratch_shapes=[pltpu.VMEM((3, E_DEV, 128), F32)],
        compiler_params=pltpu.CompilerParams(vmem_limit_bytes=4 * MIB),
        name="finish",
    )(source, time_parts, space)


def per_device(
    harmonic_state,
    direction,
    source,
    jacobian,
    frequency,
    viscosity,
    quad_weight,
    partner_device,
    partner_face,
    local_face,
    weight_index,
):
    send, elem = prep(harmonic_state, direction)

    def over_space(x, turn):
        return lax.ppermute(x, "space", [(i, (i + turn) % N_SPACE) for i in range(N_SPACE)])

    left, right, across = over_space(elem, 1), over_space(elem, -1), over_space(elem, 4)
    received = lax.all_to_all(send, "inst", 0, 0, tiled=True)
    back, to_right, to_left = spectral_sum(frequency, viscosity, received, elem, left, right, across)
    lefts, rights = over_space(to_right, 2), over_space(to_left, -2)
    time_terms = lax.all_to_all(back, "inst", 0, 0, tiled=True)
    jac_terms = jacobian_product(jacobian, elem, to_right)
    space = space_terms(
        lax.axis_index("space").reshape(1),
        quad_weight,
        partner_device.reshape(1, SLOTS_DEV),
        partner_face,
        local_face,
        weight_index,
        jac_terms,
        elem,
        (left, right, across, lefts, rights),
    )
    residual, product = finish(source.reshape(ROWS, 128), time_terms, space)
    return residual.reshape(1, FLAT), product.reshape(1, FLAT)


def solution(mesh):
    in_specs = (
        P("inst", "space"),
        P("inst", "space"),
        P("inst", "space"),
        P("inst", "space", None),
        P(),
        P(),
        P(),
        P("inst", "space", None),
        P("inst", "space"),
        P("inst", "space"),
        P("inst", "space"),
    )
    out_specs = (P("inst", "space"), P("inst", "space"))
    return jax.shard_map(
        per_device, mesh=mesh, in_specs=in_specs, out_specs=out_specs, check_vma=False
    )
```

```python
import jax
import jax.numpy as jnp
import numpy as np
from jax import lax
from jax.experimental import pallas as pl
from jax.experimental.pallas import tpu as pltpu
from jax.sharding import PartitionSpec as P

VARS = 5
PNODE = 4
E_DEV = 48
DOF = 320
SLOTS_DEV = 192
N_SPACE = 8
NT = 32
FLAT = E_DEV * DOF
ROWS = FLAT // 128
CHUNKS = 5
GROUPS = 16
BLOCK = 16
PIECE = GROUPS * 4 * DOF
MIB = 1024 * 1024
F32 = jnp.float32
BF16 = jnp.bfloat16


def face_selector():
    table = np.zeros((DOF, 6 * 128), np.float32)
    for face in range(6):
        fixed = 0 if face % 2 == 0 else PNODE - 1
        for comp in range(VARS):
            for first in range(PNODE):
                for second in range(PNODE):
                    if face < 2:
                        i, j, k = fixed, first, second
                    elif face < 4:
                        i, j, k = first, fixed, second
                    else:
                        i, j, k = first, second, fixed
                    table[comp * 64 + i * 16 + j * 4 + k, face * 128 + comp * 16 + first * 4 + second] = 1.0
    return table


def face_incidence():
    rows = np.zeros((8, 384), np.float32)
    for face in range(6):
        rows[face, :DOF] = face_selector()[:, face * 128 : (face + 1) * 128].sum(axis=1)
    return rows


def lane_half(rows):
    return lax.broadcasted_iota(jnp.int32, (rows, 128), 1) < 64


def swap(x):
    return pltpu.roll(x, 64, 1)


def join(low, high):
    return jnp.where(lane_half(low.shape[0]), swap(low), swap(high))


def first_kernel(mark_ref):
    mark_ref[...] = jnp.zeros((8, 128), F32)


def first():
    return pl.pallas_call(
        first_kernel,
        out_shape=jax.ShapeDtypeStruct((8, 128), F32),
        out_specs=pl.BlockSpec(memory_space=pltpu.VMEM),
        compiler_params=pltpu.CompilerParams(vmem_limit_bytes=MIB),
        cost_estimate=pl.CostEstimate(flops=4 * 10**9, bytes_accessed=0, transcendentals=0),
        name="first",
    )()


def prep_kernel(mark_ref, s_ref, d_ref, lin_ref, elem_ref, flat, wide):
    for k, ref in enumerate((s_ref, d_ref)):
        for r in range(ROWS):
            flat[k * ROWS + r : k * ROWS + r + 1, :] = ref[0:1, r * 128 : (r + 1) * 128].astype(F32)
    flat[2 * ROWS : 256, :] = jnp.zeros((256 - 2 * ROWS, 128), F32)
    lin_ref[...] = flat[...].astype(BF16)
    half = E_DEV // 2
    low = lane_half(half)
    s = [flat[pl.ds(q, half, stride=5), :] for q in range(5)]
    d = [flat[pl.ds(ROWS + q, half, stride=5), :] for q in range(5)]
    even = [s[0], s[1], jnp.where(low, s[2], swap(d[0])), join(d[0], d[1]), join(d[1], d[2])]
    odd = [join(s[2], s[3]), join(s[3], s[4]), jnp.where(low, swap(s[4]), d[2]), d[3], d[4]]
    for q in range(5):
        wide[q, pl.ds(0, half, stride=2), :] = even[q]
        wide[q, pl.ds(1, half, stride=2), :] = odd[q]
    for q in range(5):
        elem_ref[:, q * 128 : (q + 1) * 128] = wide[q].astype(BF16)


def prep(mark, state, direction):
    vmem = pl.BlockSpec(memory_space=pltpu.VMEM)
    return pl.pallas_call(
        prep_kernel,
        out_shape=(
            jax.ShapeDtypeStruct((256, 128), BF16),
            jax.ShapeDtypeStruct((E_DEV, 2 * DOF), BF16),
        ),
        in_specs=[pl.BlockSpec(memory_space=pl.ANY), vmem, vmem],
        out_specs=(vmem, vmem),
        scratch_shapes=[pltpu.VMEM((256, 128), F32), pltpu.VMEM((5, E_DEV, 128), F32)],
        compiler_params=pltpu.CompilerParams(vmem_limit_bytes=4 * MIB),
        name="prep",
    )(mark, state, direction)


def hand_on_kernel(x_ref, y_ref):
    y_ref[...] = x_ref[...]


def hand_on(x):
    vmem = pl.BlockSpec(memory_space=pltpu.VMEM)
    return pl.pallas_call(
        hand_on_kernel,
        out_shape=jax.ShapeDtypeStruct(x.shape, x.dtype),
        in_specs=[vmem],
        out_specs=vmem,
        compiler_params=pltpu.CompilerParams(vmem_limit_bytes=MIB),
        cost_estimate=pl.CostEstimate(flops=10**10, bytes_accessed=0, transcendentals=0),
        name="hand_on",
    )(x)


def pair_kernel(own_ref, across_ref, pair_ref):
    pair_ref[:E_DEV, :] = own_ref[...]
    pair_ref[E_DEV:, :] = across_ref[...]


def make_pair(own, across):
    vmem = pl.BlockSpec(memory_space=pltpu.VMEM)
    return pl.pallas_call(
        pair_kernel,
        out_shape=jax.ShapeDtypeStruct((2 * E_DEV, 2 * DOF), BF16),
        in_specs=[vmem, vmem],
        out_specs=vmem,
        compiler_params=pltpu.CompilerParams(vmem_limit_bytes=2 * MIB),
        name="pair",
    )(own, across)


def circulant_parts():
    j = np.arange(1, NT)
    sign = 1.0 - 2.0 * (j % 2)
    angle = np.pi * j / NT
    first = np.concatenate([[0.0], 0.5 * sign * np.cos(angle) / np.sin(angle)])
    second = np.concatenate([[-(NT * NT + 2) / 12.0], -sign / (2.0 * np.sin(angle) ** 2)])
    return first, second


def spectral_kernel(freq_ref, visc_ref, x_ref, after_ref, y_ref):
    first, second = circulant_parts()
    freq, visc = freq_ref[...], visc_ref[...]
    half = NT // 2
    x = x_ref[...].astype(F32).reshape(NT, 8, 128)

    def coef(a, b):
        return jnp.broadcast_to(freq * float(a) + visc * float(b), (8, 128))

    def part(sgn):
        c = [
            coef(0.5 * (first[j] + sgn * first[j + half]), 0.5 * (second[j] + sgn * second[j + half]))
            for j in range(half)
        ]
        u = [x[s] + sgn * x[s + half] for s in range(half)]
        out = []
        for t in range(half):
            acc = None
            for s in range(half):
                j = t - s
                term = c[j % half] * u[s]
                if acc is None:
                    acc = term
                elif j < 0 and sgn < 0:
                    acc = acc - term
                else:
                    acc = acc + term
            out.append(acc)
        return out

    even = part(1.0)
    for t in range(half):
        y_ref[t * 8 : (t + 1) * 8, :] = even[t]
    odd = part(-1.0)
    for t in range(half):
        e = y_ref[t * 8 : (t + 1) * 8, :]
        y_ref[t * 8 : (t + 1) * 8, :] = e + odd[t]
        y_ref[(t + half) * 8 : (t + half + 1) * 8, :] = e - odd[t]


def spectral_sum(frequency, viscosity, received, after):
    vmem = pl.BlockSpec(memory_space=pltpu.VMEM)
    return pl.pallas_call(
        spectral_kernel,
        out_shape=jax.ShapeDtypeStruct((256, 128), F32),
        in_specs=[vmem] * 3 + [pl.BlockSpec(memory_space=pl.ANY)],
        out_specs=vmem,
        compiler_params=pltpu.CompilerParams(vmem_limit_bytes=4 * MIB),
        cost_estimate=pl.CostEstimate(flops=10**10, bytes_accessed=0, transcendentals=0),
        name="spectral",
    )(frequency.reshape(1, 1), viscosity.reshape(1, 1), received, after)


def vector_tiles(elem):
    p = [elem[:, q * 128 : (q + 1) * 128] for q in range(5)]
    low = lane_half(E_DEV)
    zero = jnp.zeros((E_DEV, 128), F32)
    s = [p[0], p[1], jnp.where(low, p[2], zero), jnp.where(low, zero, swap(p[0])), join(p[0], p[1]), join(p[1], p[2])]
    d = [join(p[2], p[3]), join(p[3], p[4]), jnp.where(low, swap(p[4]), zero), jnp.where(low, zero, p[2]), p[3], p[4]]
    return s, d


def jacobian_kernel(jac_ref, elem_ref, after_ref, out_ref, weights, acc, rows):
    s, d = vector_tiles(elem_ref[...].astype(F32))
    pad = jnp.zeros((128 - 2 * E_DEV, 128), F32)
    blocks = E_DEV // BLOCK
    turned = []
    for q in range(3):
        parts = []
        for b in range(blocks):
            parts += [s[q][b * BLOCK : (b + 1) * BLOCK], d[q][b * BLOCK : (b + 1) * BLOCK]]
        turned.append(jnp.concatenate(parts + [pad], axis=0).T)
    turned = jnp.concatenate(turned, axis=0)[:DOF]
    lane = lax.broadcasted_iota(jnp.int32, (DOF, 128), 1)
    for b in range(blocks):
        for i in range(4):
            at = turned if i == b else pltpu.roll(turned, (i - b) * 32 % 128, 1)
            at = jnp.where((lane >= 32 * i) & (lane < 32 * (i + 1)), at, 0.0)
            weights[b, DOF * i : DOF * (i + 1), :] = at.astype(BF16)
    e = lax.broadcasted_iota(jnp.int32, (BLOCK, 128), 0)
    keep = (lax.broadcasted_iota(jnp.int32, (BLOCK, 128), 1) & (BLOCK - 1)) == e

    def step(c, carry):
        for b in range(blocks):
            lhs = jnp.concatenate(
                [
                    jac_ref[0, b * BLOCK : (b + 1) * BLOCK, pl.ds(pl.multiple_of(c * PIECE, PIECE) + g * 4 * DOF, 4 * DOF)]
                    for g in range(GROUPS)
                ],
                axis=0,
            )
            res = jnp.dot(lhs, weights[b], preferred_element_type=F32)
            res = jnp.where(keep[None], res.reshape(GROUPS, BLOCK, 128), 0.0)
            acc[b, pl.ds(pl.multiple_of(c * GROUPS, GROUPS), GROUPS), :] = jnp.sum(res, axis=1)
        return carry

    lax.fori_loop(0, CHUNKS, step, 0)
    groups = CHUNKS * GROUPS
    lane = lax.broadcasted_iota(jnp.int32, (groups, 128), 1)
    for i in range(4):
        at = jnp.zeros((groups, 128), F32)
        for b in range(blocks):
            moved = acc[b] if i == b else pltpu.roll(acc[b], (b - i) * 32 % 128, 1)
            at = jnp.where((lane >= 32 * b) & (lane < 32 * (b + 1)), moved, at)
        rows[pl.ds(i, groups, stride=4), :] = at
    rows[DOF:, :] = jnp.zeros((384 - DOF, 128), F32)
    for q in range(3):
        back = rows[q * 128 : (q + 1) * 128, :].T
        for b in range(blocks):
            for k in range(2):
                out_ref[k * E_DEV + b * BLOCK : k * E_DEV + (b + 1) * BLOCK, q * 128 : (q + 1) * 128] = back[
                    b * 32 + k * BLOCK : b * 32 + (k + 1) * BLOCK
                ]


def jacobian_product(jacobian, elem, after):
    return pl.pallas_call(
        jacobian_kernel,
        out_shape=jax.ShapeDtypeStruct((2 * E_DEV, 384), F32),
        in_specs=[
            pl.BlockSpec(memory_space=pltpu.VMEM),
            pl.BlockSpec(memory_space=pltpu.VMEM),
            pl.BlockSpec(memory_space=pl.ANY),
        ],
        out_specs=pl.BlockSpec(memory_space=pltpu.VMEM),
        scratch_shapes=[
            pltpu.VMEM((E_DEV // BLOCK, 4 * DOF, 128), BF16),
            pltpu.VMEM((E_DEV // BLOCK, CHUNKS * GROUPS, 128), F32),
            pltpu.VMEM((384, 128), F32),
        ],
        compiler_params=pltpu.CompilerParams(vmem_limit_bytes=8 * MIB),
        cost_estimate=pl.CostEstimate(
            flops=2 * 2 * E_DEV * DOF * DOF * 48, bytes_accessed=2 * E_DEV * DOF * DOF, transcendentals=0
        ),
        name="jacobian",
    )(jacobian, elem, after)


def split(x):
    high = x.astype(BF16)
    return high, (x - high.astype(F32)).astype(BF16)


def flux_kernel(
    quad_ref, dev_ref, far_ref, near_ref, cls_ref, jac_ref, sel_ref, inc_ref, elem_ref, *rest
):
    tables, out_ref = rest[:-1], rest[-1]
    me = lax.axis_index("space")
    far = far_ref[...]
    near = near_ref[...]
    cls = cls_ref[...]
    far_e = (far * 10923) >> 16
    far_l = far - far_e * 6
    near_e = (near * 10923) >> 16
    near_row = (near - near_e * 6) * E_DEV + near_e
    turn = (dev_ref[...] - me) & (N_SPACE - 1)
    block = jnp.zeros((1, SLOTS_DEV), jnp.int32)
    for at, which in enumerate((0, 4, 7, 3, 1, 5, 6, 2)):
        block = jnp.where(turn == which, at, block)
    column = block * E_DEV + far_e
    w = jnp.zeros((1, SLOTS_DEV), F32)
    for c in range(16):
        w = jnp.where(cls == c, quad_ref[:, c : c + 1], w)
    r = lax.broadcasted_iota(jnp.int32, (SLOTS_DEV, SLOTS_DEV), 0)
    c = lax.broadcasted_iota(jnp.int32, (SLOTS_DEV, SLOTS_DEV), 1)
    both = (far_l * 512 + column).astype(F32)
    code = jnp.sum(jnp.where(r == c, both, 0.0), axis=1, keepdims=True).astype(jnp.int32)
    column_s = code & 511
    far_ls = code >> 9
    total = N_SPACE * E_DEV
    pick = (lax.broadcasted_iota(jnp.int32, (SLOTS_DEV, total), 1) == column_s).astype(F32).astype(BF16)
    table = jnp.concatenate([t[...] for t in tables], axis=0)
    got = jnp.dot(pick, table, preferred_element_type=F32)
    p = [got[:, q * 128 : (q + 1) * 128] for q in range(5)]
    low = lane_half(SLOTS_DEV)
    zero = jnp.zeros((SLOTS_DEV, 128), F32)
    fields = jnp.concatenate(
        [
            jnp.concatenate([p[0], p[1], jnp.where(low, p[2], zero)], axis=1),
            jnp.concatenate([join(p[2], p[3]), join(p[3], p[4]), jnp.where(low, swap(p[4]), zero)], axis=1),
        ],
        axis=0,
    ).astype(BF16)
    sel = sel_ref[...]
    faces = jnp.dot(fields, sel, preferred_element_type=F32)
    which = jnp.concatenate([far_ls, far_ls], axis=0)
    trace = jnp.zeros((2 * SLOTS_DEV, 128), F32)
    for face in range(6):
        trace = jnp.where(which == face, faces[:, face * 128 : (face + 1) * 128], trace)
    trace = jnp.concatenate([trace[:SLOTS_DEV], trace[SLOTS_DEV:]], axis=1).astype(BF16)
    rows = lax.broadcasted_iota(jnp.int32, (6 * E_DEV, SLOTS_DEV), 0)
    spread = jnp.where(rows == near_row, w, 0.0)
    high, rest_w = split(spread)
    flux = jnp.dot(high, trace, preferred_element_type=F32) + jnp.dot(rest_w, trace, preferred_element_type=F32)
    weight_sum = jnp.sum(spread, axis=1, keepdims=True)
    lhs = jnp.concatenate(
        [
            jnp.concatenate(
                [flux[f * E_DEV : (f + 1) * E_DEV, :128], flux[f * E_DEV : (f + 1) * E_DEV, 128:]], axis=0
            )
            for f in range(6)
        ],
        axis=1,
    )
    high, rest_f = split(lhs)
    dims = (((1,), (1,)), ((), ()))
    lifted = lax.dot_general(high, sel, dims, preferred_element_type=F32) + lax.dot_general(
        rest_f, sel, dims, preferred_element_type=F32
    )
    coef = jnp.zeros((E_DEV, 384), F32)
    for f in range(6):
        coef = coef + weight_sum[f * E_DEV : (f + 1) * E_DEV] * inc_ref[f : f + 1, :]
    fields_own = vector_tiles(elem_ref[...].astype(F32))
    for k in range(2):
        own = jnp.concatenate(fields_own[k][:3], axis=1)
        rows_k = slice(k * E_DEV, (k + 1) * E_DEV)
        out_ref[rows_k, :] = jac_ref[rows_k, :] + coef * own - lifted[rows_k]


def space_terms(quad, dev, far, near, cls, jac_terms, elem, tables):
    sel = np.zeros((384, 768), np.float32)
    sel[:DOF] = face_selector()
    vmem = pl.BlockSpec(memory_space=pltpu.VMEM)
    return pl.pallas_call(
        flux_kernel,
        out_shape=jax.ShapeDtypeStruct((2 * E_DEV, 384), F32),
        in_specs=[vmem] * (9 + len(tables)),
        out_specs=vmem,
        compiler_params=pltpu.CompilerParams(vmem_limit_bytes=12 * MIB),
        name="space_terms",
    )(
        quad.reshape(1, 16), dev, far, near, cls, jac_terms,
        jnp.asarray(sel, BF16), jnp.asarray(face_incidence()), elem, *tables,
    )


def final_kernel(src_ref, time_ref, space_ref, res_ref, prod_ref, scratch):
    half = E_DEV // 2
    low = lane_half(half)
    for k, out_ref in enumerate((res_ref, prod_ref)):
        for q in range(3):
            scratch[q] = space_ref[k * E_DEV : (k + 1) * E_DEV, q * 128 : (q + 1) * 128]
        even = [scratch[q, pl.ds(0, half, stride=2), :] for q in range(3)]
        odd = [scratch[q, pl.ds(1, half, stride=2), :] for q in range(3)]
        tiles = [
            even[0],
            even[1],
            jnp.where(low, even[2], swap(odd[0])),
            join(odd[0], odd[1]),
            join(odd[1], odd[2]),
        ]
        for q in range(5):
            at = time_ref[pl.ds(k * ROWS + q, half, stride=5), :] + tiles[q]
            if k == 0:
                at = src_ref[pl.ds(q, half, stride=5), :] - at
            out_ref[pl.ds(q, half, stride=5), :] = at


def finish(source, time_parts, space):
    vmem = pl.BlockSpec(memory_space=pltpu.VMEM)
    return pl.pallas_call(
        final_kernel,
        out_shape=(jax.ShapeDtypeStruct((ROWS, 128), F32),) * 2,
        in_specs=[vmem] * 3,
        out_specs=(vmem, vmem),
        scratch_shapes=[pltpu.VMEM((3, E_DEV, 128), F32)],
        compiler_params=pltpu.CompilerParams(vmem_limit_bytes=4 * MIB),
        name="finish",
    )(source, time_parts, space)


def per_device(
    harmonic_state,
    direction,
    source,
    jacobian,
    frequency,
    viscosity,
    quad_weight,
    partner_device,
    partner_face,
    local_face,
    weight_index,
):
    lin, elem = prep(first(), harmonic_state, direction)

    def over_space(x, turn):
        return lax.ppermute(x, "space", [(i, (i + turn) % N_SPACE) for i in range(N_SPACE)])

    across = over_space(elem, 4)
    received = lax.all_to_all(hand_on(lin), "inst", 0, 0, tiled=True)
    pair = make_pair(elem, across)
    others = [over_space(pair, turn) for turn in (1, -1, 2)]
    back = spectral_sum(frequency, viscosity, received, pair)
    time_terms = lax.all_to_all(back, "inst", 0, 0, tiled=True)
    jac_terms = jacobian_product(jacobian, elem, back)
    space = space_terms(
        quad_weight,
        partner_device.reshape(1, SLOTS_DEV),
        partner_face,
        local_face,
        weight_index,
        jac_terms,
        elem,
        [pair] + others,
    )
    residual, product = finish(source.reshape(ROWS, 128), time_terms, space)
    return residual.reshape(1, FLAT), product.reshape(1, FLAT)


def solution(mesh):
    in_specs = (
        P("inst", "space"),
        P("inst", "space"),
        P("inst", "space"),
        P("inst", "space", None),
        P(),
        P(),
        P(),
        P("inst", "space", None),
        P("inst", "space"),
        P("inst", "space"),
        P("inst", "space"),
    )
    out_specs = (P("inst", "space"), P("inst", "space"))
    return jax.shard_map(
        per_device, mesh=mesh, in_specs=in_specs, out_specs=out_specs, check_vma=False
    )
```

```python
import jax
import jax.numpy as jnp
import numpy as np
from jax import lax
from jax.experimental import pallas as pl
from jax.experimental.pallas import tpu as pltpu
from jax.sharding import PartitionSpec as P

VARS = 5
PNODE = 4
E_DEV = 48
DOF = 320
SLOTS_DEV = 192
N_SPACE = 8
NT = 32
FLAT = E_DEV * DOF
ROWS = FLAT // 128
CHUNKS = 10
GROUPS = 8
BLOCK = 16
PIECE = GROUPS * 4 * DOF
SPARE = 16
MIB = 1024 * 1024
F32 = jnp.float32
BF16 = jnp.bfloat16


def face_selector():
    table = np.zeros((DOF, 6 * 128), np.float32)
    for face in range(6):
        fixed = 0 if face % 2 == 0 else PNODE - 1
        for comp in range(VARS):
            for first in range(PNODE):
                for second in range(PNODE):
                    if face < 2:
                        i, j, k = fixed, first, second
                    elif face < 4:
                        i, j, k = first, fixed, second
                    else:
                        i, j, k = first, second, fixed
                    table[comp * 64 + i * 16 + j * 4 + k, face * 128 + comp * 16 + first * 4 + second] = 1.0
    return table


def face_incidence():
    rows = np.zeros((8, 384), np.float32)
    for face in range(6):
        rows[face, :DOF] = face_selector()[:, face * 128 : (face + 1) * 128].sum(axis=1)
    return rows


def lane_half(rows):
    return lax.broadcasted_iota(jnp.int32, (rows, 128), 1) < 64


def swap(x):
    return pltpu.roll(x, 64, 1)


def join(low, high):
    return jnp.where(lane_half(low.shape[0]), swap(low), swap(high))


def first_kernel(mark_ref):
    mark_ref[...] = jnp.zeros((8, 128), F32)


def first():
    return pl.pallas_call(
        first_kernel,
        out_shape=jax.ShapeDtypeStruct((8, 128), F32),
        out_specs=pl.BlockSpec(memory_space=pltpu.VMEM),
        compiler_params=pltpu.CompilerParams(vmem_limit_bytes=MIB),
        cost_estimate=pl.CostEstimate(flops=4 * 10**9, bytes_accessed=0, transcendentals=0),
        name="first",
    )()


def prep_kernel(mark_ref, s_ref, d_ref, lin_ref, elem_ref, flat, wide):
    for k, ref in enumerate((s_ref, d_ref)):
        for r in range(ROWS):
            flat[k * ROWS + r : k * ROWS + r + 1, :] = ref[0:1, r * 128 : (r + 1) * 128].astype(F32)
    flat[2 * ROWS : 256, :] = jnp.zeros((256 - 2 * ROWS, 128), F32)
    lin_ref[...] = flat[...].astype(BF16)
    half = E_DEV // 2
    low = lane_half(half)
    s = [flat[pl.ds(q, half, stride=5), :] for q in range(5)]
    d = [flat[pl.ds(ROWS + q, half, stride=5), :] for q in range(5)]
    even = [s[0], s[1], jnp.where(low, s[2], swap(d[0])), join(d[0], d[1]), join(d[1], d[2])]
    odd = [join(s[2], s[3]), join(s[3], s[4]), jnp.where(low, swap(s[4]), d[2]), d[3], d[4]]
    for q in range(5):
        wide[q, pl.ds(0, half, stride=2), :] = even[q]
        wide[q, pl.ds(1, half, stride=2), :] = odd[q]
    for q in range(5):
        elem_ref[:E_DEV, q * 128 : (q + 1) * 128] = wide[q].astype(BF16)
    elem_ref[E_DEV:, :] = jnp.zeros((SPARE, 2 * DOF), BF16)


def prep(mark, state, direction):
    vmem = pl.BlockSpec(memory_space=pltpu.VMEM)
    return pl.pallas_call(
        prep_kernel,
        out_shape=(
            jax.ShapeDtypeStruct((256, 128), BF16),
            jax.ShapeDtypeStruct((E_DEV + SPARE, 2 * DOF), BF16),
        ),
        in_specs=[pl.BlockSpec(memory_space=pl.ANY), vmem, vmem],
        out_specs=(vmem, vmem),
        scratch_shapes=[pltpu.VMEM((256, 128), F32), pltpu.VMEM((5, E_DEV, 128), F32)],
        compiler_params=pltpu.CompilerParams(vmem_limit_bytes=4 * MIB),
        name="prep",
    )(mark, state, direction)


def pair_kernel(own_ref, across_ref, pair_ref):
    pair_ref[:E_DEV, :] = own_ref[:E_DEV, :]
    pair_ref[E_DEV : 2 * E_DEV, :] = across_ref[:E_DEV, :]
    pair_ref[2 * E_DEV :, :] = jnp.zeros((SPARE, 2 * DOF), BF16)


def make_pair(own, across):
    vmem = pl.BlockSpec(memory_space=pltpu.VMEM)
    return pl.pallas_call(
        pair_kernel,
        out_shape=jax.ShapeDtypeStruct((2 * E_DEV + SPARE, 2 * DOF), BF16),
        in_specs=[vmem, vmem],
        out_specs=vmem,
        compiler_params=pltpu.CompilerParams(vmem_limit_bytes=2 * MIB),
        name="pair",
    )(own, across)


def circulant_parts():
    j = np.arange(1, NT)
    sign = 1.0 - 2.0 * (j % 2)
    angle = np.pi * j / NT
    first = np.concatenate([[0.0], 0.5 * sign * np.cos(angle) / np.sin(angle)])
    second = np.concatenate([[-(NT * NT + 2) / 12.0], -sign / (2.0 * np.sin(angle) ** 2)])
    return first, second


def spectral_kernel(freq_ref, visc_ref, x_ref, after_ref, y_ref):
    first, second = circulant_parts()
    freq, visc = freq_ref[...], visc_ref[...]
    half = NT // 2
    x = x_ref[...].astype(F32).reshape(NT, 8, 128)

    def coef(a, b):
        return jnp.broadcast_to(freq * float(a) + visc * float(b), (8, 128))

    def part(sgn):
        c = [
            coef(0.5 * (first[j] + sgn * first[j + half]), 0.5 * (second[j] + sgn * second[j + half]))
            for j in range(half)
        ]
        u = [x[s] + sgn * x[s + half] for s in range(half)]
        out = []
        for t in range(half):
            acc = None
            for s in range(half):
                j = t - s
                term = c[j % half] * u[s]
                if acc is None:
                    acc = term
                elif j < 0 and sgn < 0:
                    acc = acc - term
                else:
                    acc = acc + term
            out.append(acc)
        return out

    even = part(1.0)
    for t in range(half):
        y_ref[t * 8 : (t + 1) * 8, :] = even[t]
    odd = part(-1.0)
    for t in range(half):
        e = y_ref[t * 8 : (t + 1) * 8, :]
        y_ref[t * 8 : (t + 1) * 8, :] = e + odd[t]
        y_ref[(t + half) * 8 : (t + half + 1) * 8, :] = e - odd[t]


def spectral_sum(frequency, viscosity, received, after):
    vmem = pl.BlockSpec(memory_space=pltpu.VMEM)
    return pl.pallas_call(
        spectral_kernel,
        out_shape=jax.ShapeDtypeStruct((256, 128), F32),
        in_specs=[vmem] * 3 + [pl.BlockSpec(memory_space=pl.ANY)],
        out_specs=vmem,
        compiler_params=pltpu.CompilerParams(vmem_limit_bytes=4 * MIB),
        cost_estimate=pl.CostEstimate(flops=10**10, bytes_accessed=0, transcendentals=0),
        name="spectral",
    )(frequency.reshape(1, 1), viscosity.reshape(1, 1), received, after)


def vector_tiles(elem):
    p = [elem[:, q * 128 : (q + 1) * 128] for q in range(5)]
    low = lane_half(E_DEV)
    zero = jnp.zeros((E_DEV, 128), F32)
    s = [p[0], p[1], jnp.where(low, p[2], zero), jnp.where(low, zero, swap(p[0])), join(p[0], p[1]), join(p[1], p[2])]
    d = [join(p[2], p[3]), join(p[3], p[4]), jnp.where(low, swap(p[4]), zero), jnp.where(low, zero, p[2]), p[3], p[4]]
    return s, d


def jacobian_kernel(jac_hbm, elem_ref, after_ref, out_ref, held, weights, acc, rows, sems):
    def piece(c, start):
        return pltpu.make_async_copy(jac_hbm.at[0, :, pl.ds(start, PIECE)], held.at[c], sems.at[c])

    for c in range(CHUNKS):
        piece(c, c * PIECE).start()
    s, d = vector_tiles(elem_ref[:E_DEV, :].astype(F32))
    pad = jnp.zeros((128 - 2 * E_DEV, 128), F32)
    blocks = E_DEV // BLOCK
    turned = []
    for q in range(3):
        parts = []
        for b in range(blocks):
            parts += [s[q][b * BLOCK : (b + 1) * BLOCK], d[q][b * BLOCK : (b + 1) * BLOCK]]
        turned.append(jnp.concatenate(parts + [pad], axis=0).T)
    turned = jnp.concatenate(turned, axis=0)[:DOF]
    lane = lax.broadcasted_iota(jnp.int32, (DOF, 128), 1)
    for b in range(blocks):
        for i in range(4):
            at = turned if i == b else pltpu.roll(turned, (i - b) * 32 % 128, 1)
            at = jnp.where((lane >= 32 * i) & (lane < 32 * (i + 1)), at, 0.0)
            weights[b, DOF * i : DOF * (i + 1), :] = at.astype(BF16)
    e = lax.broadcasted_iota(jnp.int32, (BLOCK, 128), 0)
    keep = (lax.broadcasted_iota(jnp.int32, (BLOCK, 128), 1) & (BLOCK - 1)) == e

    def step(c, carry):
        piece(c, pl.multiple_of(c * PIECE, PIECE)).wait()
        for b in range(blocks):
            lhs = jnp.concatenate(
                [
                    held[c, b * BLOCK : (b + 1) * BLOCK, g * 4 * DOF : (g + 1) * 4 * DOF]
                    for g in range(GROUPS)
                ],
                axis=0,
            )
            res = jnp.dot(lhs, weights[b], preferred_element_type=F32)
            res = jnp.where(keep[None], res.reshape(GROUPS, BLOCK, 128), 0.0)
            acc[b, pl.ds(pl.multiple_of(c * GROUPS, GROUPS), GROUPS), :] = jnp.sum(res, axis=1)
        return carry

    lax.fori_loop(0, CHUNKS, step, 0)
    groups = CHUNKS * GROUPS
    lane = lax.broadcasted_iota(jnp.int32, (groups, 128), 1)
    for i in range(4):
        at = jnp.zeros((groups, 128), F32)
        for b in range(blocks):
            moved = acc[b] if i == b else pltpu.roll(acc[b], (b - i) * 32 % 128, 1)
            at = jnp.where((lane >= 32 * b) & (lane < 32 * (b + 1)), moved, at)
        rows[pl.ds(i, groups, stride=4), :] = at
    rows[DOF:, :] = jnp.zeros((384 - DOF, 128), F32)
    for q in range(3):
        back = rows[q * 128 : (q + 1) * 128, :].T
        for b in range(blocks):
            for k in range(2):
                out_ref[k * E_DEV + b * BLOCK : k * E_DEV + (b + 1) * BLOCK, q * 128 : (q + 1) * 128] = back[
                    b * 32 + k * BLOCK : b * 32 + (k + 1) * BLOCK
                ]


def jacobian_product(jacobian, elem, after):
    return pl.pallas_call(
        jacobian_kernel,
        out_shape=jax.ShapeDtypeStruct((2 * E_DEV, 384), F32),
        in_specs=[
            pl.BlockSpec(memory_space=pltpu.HBM),
            pl.BlockSpec(memory_space=pltpu.VMEM),
            pl.BlockSpec(memory_space=pl.ANY),
        ],
        out_specs=pl.BlockSpec(memory_space=pltpu.VMEM),
        scratch_shapes=[
            pltpu.VMEM((CHUNKS, E_DEV, PIECE), BF16),
            pltpu.VMEM((E_DEV // BLOCK, 4 * DOF, 128), BF16),
            pltpu.VMEM((E_DEV // BLOCK, CHUNKS * GROUPS, 128), F32),
            pltpu.VMEM((384, 128), F32),
            pltpu.SemaphoreType.DMA((CHUNKS,)),
        ],
        compiler_params=pltpu.CompilerParams(vmem_limit_bytes=49 * MIB),
        cost_estimate=pl.CostEstimate(
            flops=2 * 2 * E_DEV * DOF * DOF * 48, bytes_accessed=2 * E_DEV * DOF * DOF, transcendentals=0
        ),
        name="jacobian",
    )(jacobian, elem, after)


def split(x):
    high = x.astype(BF16)
    return high, (x - high.astype(F32)).astype(BF16)


def flux_kernel(
    quad_ref, dev_ref, far_ref, near_ref, cls_ref, jac_ref, sel_ref, inc_ref, elem_ref, *rest
):
    tables, out_ref = rest[:-1], rest[-1]
    me = lax.axis_index("space")
    far = far_ref[...]
    near = near_ref[...]
    cls = cls_ref[...]
    far_e = (far * 10923) >> 16
    far_l = far - far_e * 6
    near_e = (near * 10923) >> 16
    near_row = (near - near_e * 6) * E_DEV + near_e
    turn = (dev_ref[...] - me) & (N_SPACE - 1)
    block = jnp.zeros((1, SLOTS_DEV), jnp.int32)
    for at, which in enumerate((0, 4, 7, 3, 1, 5, 6, 2)):
        block = jnp.where(turn == which, at, block)
    column = block * E_DEV + far_e
    w = jnp.zeros((1, SLOTS_DEV), F32)
    for c in range(16):
        w = jnp.where(cls == c, quad_ref[:, c : c + 1], w)
    r = lax.broadcasted_iota(jnp.int32, (SLOTS_DEV, SLOTS_DEV), 0)
    c = lax.broadcasted_iota(jnp.int32, (SLOTS_DEV, SLOTS_DEV), 1)
    both = (far_l * 512 + column).astype(F32)
    code = jnp.sum(jnp.where(r == c, both, 0.0), axis=1, keepdims=True).astype(jnp.int32)
    column_s = code & 511
    far_ls = code >> 9
    total = N_SPACE * E_DEV
    pick = (lax.broadcasted_iota(jnp.int32, (SLOTS_DEV, total), 1) == column_s).astype(F32).astype(BF16)
    table = jnp.concatenate([t[: 2 * E_DEV, :] for t in tables], axis=0)
    got = jnp.dot(pick, table, preferred_element_type=F32)
    p = [got[:, q * 128 : (q + 1) * 128] for q in range(5)]
    low = lane_half(SLOTS_DEV)
    zero = jnp.zeros((SLOTS_DEV, 128), F32)
    fields = jnp.concatenate(
        [
            jnp.concatenate([p[0], p[1], jnp.where(low, p[2], zero)], axis=1),
            jnp.concatenate([join(p[2], p[3]), join(p[3], p[4]), jnp.where(low, swap(p[4]), zero)], axis=1),
        ],
        axis=0,
    ).astype(BF16)
    sel = sel_ref[...]
    faces = jnp.dot(fields, sel, preferred_element_type=F32)
    which = jnp.concatenate([far_ls, far_ls], axis=0)
    trace = jnp.zeros((2 * SLOTS_DEV, 128), F32)
    for face in range(6):
        trace = jnp.where(which == face, faces[:, face * 128 : (face + 1) * 128], trace)
    trace = jnp.concatenate([trace[:SLOTS_DEV], trace[SLOTS_DEV:]], axis=1).astype(BF16)
    rows = lax.broadcasted_iota(jnp.int32, (6 * E_DEV, SLOTS_DEV), 0)
    spread = jnp.where(rows == near_row, w, 0.0)
    high, rest_w = split(spread)
    flux = jnp.dot(high, trace, preferred_element_type=F32) + jnp.dot(rest_w, trace, preferred_element_type=F32)
    weight_sum = jnp.sum(spread, axis=1, keepdims=True)
    lhs = jnp.concatenate(
        [
            jnp.concatenate(
                [flux[f * E_DEV : (f + 1) * E_DEV, :128], flux[f * E_DEV : (f + 1) * E_DEV, 128:]], axis=0
            )
            for f in range(6)
        ],
        axis=1,
    )
    high, rest_f = split(lhs)
    dims = (((1,), (1,)), ((), ()))
    lifted = lax.dot_general(high, sel, dims, preferred_element_type=F32) + lax.dot_general(
        rest_f, sel, dims, preferred_element_type=F32
    )
    coef = jnp.zeros((E_DEV, 384), F32)
    for f in range(6):
        coef = coef + weight_sum[f * E_DEV : (f + 1) * E_DEV] * inc_ref[f : f + 1, :]
    fields_own = vector_tiles(elem_ref[:E_DEV, :].astype(F32))
    for k in range(2):
        own = jnp.concatenate(fields_own[k][:3], axis=1)
        rows_k = slice(k * E_DEV, (k + 1) * E_DEV)
        out_ref[rows_k, :] = jac_ref[rows_k, :] + coef * own - lifted[rows_k]


def space_terms(quad, dev, far, near, cls, jac_terms, elem, tables):
    sel = np.zeros((384, 768), np.float32)
    sel[:DOF] = face_selector()
    vmem = pl.BlockSpec(memory_space=pltpu.VMEM)
    return pl.pallas_call(
        flux_kernel,
        out_shape=jax.ShapeDtypeStruct((2 * E_DEV, 384), F32),
        in_specs=[vmem] * (9 + len(tables)),
        out_specs=vmem,
        compiler_params=pltpu.CompilerParams(vmem_limit_bytes=12 * MIB),
        name="space_terms",
    )(
        quad.reshape(1, 16), dev, far, near, cls, jac_terms,
        jnp.asarray(sel, BF16), jnp.asarray(face_incidence()), elem, *tables,
    )


def final_kernel(src_ref, time_ref, space_ref, res_ref, prod_ref, scratch):
    half = E_DEV // 2
    low = lane_half(half)
    for k, out_ref in enumerate((res_ref, prod_ref)):
        for q in range(3):
            scratch[q] = space_ref[k * E_DEV : (k + 1) * E_DEV, q * 128 : (q + 1) * 128]
        even = [scratch[q, pl.ds(0, half, stride=2), :] for q in range(3)]
        odd = [scratch[q, pl.ds(1, half, stride=2), :] for q in range(3)]
        tiles = [
            even[0],
            even[1],
            jnp.where(low, even[2], swap(odd[0])),
            join(odd[0], odd[1]),
            join(odd[1], odd[2]),
        ]
        for q in range(5):
            at = time_ref[pl.ds(k * ROWS + q, half, stride=5), :] + tiles[q]
            if k == 0:
                at = src_ref[pl.ds(q, half, stride=5), :] - at
            out_ref[pl.ds(q, half, stride=5), :] = at


def finish(source, time_parts, space):
    vmem = pl.BlockSpec(memory_space=pltpu.VMEM)
    return pl.pallas_call(
        final_kernel,
        out_shape=(jax.ShapeDtypeStruct((ROWS, 128), F32),) * 2,
        in_specs=[vmem] * 3,
        out_specs=(vmem, vmem),
        scratch_shapes=[pltpu.VMEM((3, E_DEV, 128), F32)],
        compiler_params=pltpu.CompilerParams(vmem_limit_bytes=4 * MIB),
        name="finish",
    )(source, time_parts, space)


def per_device(
    harmonic_state,
    direction,
    source,
    jacobian,
    frequency,
    viscosity,
    quad_weight,
    partner_device,
    partner_face,
    local_face,
    weight_index,
):
    lin, elem = prep(first(), harmonic_state, direction)

    def over_space(x, turn):
        return lax.ppermute(x, "space", [(i, (i + turn) % N_SPACE) for i in range(N_SPACE)])

    across = over_space(elem, 4)
    received = lax.all_to_all(lin, "inst", 0, 0, tiled=True)
    pair = make_pair(elem, across)
    others = [over_space(pair, turn) for turn in (1, -1, 2)]
    back = spectral_sum(frequency, viscosity, received, pair)
    time_terms = lax.all_to_all(back, "inst", 0, 0, tiled=True)
    jac_terms = jacobian_product(jacobian, elem, back)
    space = space_terms(
        quad_weight,
        partner_device.reshape(1, SLOTS_DEV),
        partner_face,
        local_face,
        weight_index,
        jac_terms,
        elem,
        [pair] + others,
    )
    residual, product = finish(source.reshape(ROWS, 128), time_terms, space)
    return residual.reshape(1, FLAT), product.reshape(1, FLAT)


def solution(mesh):
    in_specs = (
        P("inst", "space"),
        P("inst", "space"),
        P("inst", "space"),
        P("inst", "space", None),
        P(),
        P(),
        P(),
        P("inst", "space", None),
        P("inst", "space"),
        P("inst", "space"),
        P("inst", "space"),
    )
    out_specs = (P("inst", "space"), P("inst", "space"))
    return jax.shard_map(
        per_device, mesh=mesh, in_specs=in_specs, out_specs=out_specs, check_vma=False
    )
```

```python
import jax
import jax.numpy as jnp
import numpy as np
from jax import lax
from jax.experimental import pallas as pl
from jax.experimental.pallas import tpu as pltpu
from jax.sharding import PartitionSpec as P

VARS = 5
PNODE = 4
E_DEV = 48
DOF = 320
SLOTS_DEV = 192
N_SPACE = 8
NT = 32
FLAT = E_DEV * DOF
ROWS = FLAT // 128
CHUNKS = 5
GROUPS = 16
BLOCK = 16
PIECE = GROUPS * 4 * DOF
SPARE = 16
MIB = 1024 * 1024
F32 = jnp.float32
BF16 = jnp.bfloat16


def face_selector():
    table = np.zeros((DOF, 6 * 128), np.float32)
    for face in range(6):
        fixed = 0 if face % 2 == 0 else PNODE - 1
        for comp in range(VARS):
            for first in range(PNODE):
                for second in range(PNODE):
                    if face < 2:
                        i, j, k = fixed, first, second
                    elif face < 4:
                        i, j, k = first, fixed, second
                    else:
                        i, j, k = first, second, fixed
                    table[comp * 64 + i * 16 + j * 4 + k, face * 128 + comp * 16 + first * 4 + second] = 1.0
    return table


def face_incidence():
    rows = np.zeros((8, 384), np.float32)
    for face in range(6):
        rows[face, :DOF] = face_selector()[:, face * 128 : (face + 1) * 128].sum(axis=1)
    return rows


def lane_half(rows):
    return lax.broadcasted_iota(jnp.int32, (rows, 128), 1) < 64


def swap(x):
    return pltpu.roll(x, 64, 1)


def join(low, high):
    return jnp.where(lane_half(low.shape[0]), swap(low), swap(high))


def circulant_parts():
    j = np.arange(1, NT)
    sign = 1.0 - 2.0 * (j % 2)
    angle = np.pi * j / NT
    first = np.concatenate([[0.0], 0.5 * sign * np.cos(angle) / np.sin(angle)])
    second = np.concatenate([[-(NT * NT + 2) / 12.0], -sign / (2.0 * np.sin(angle) ** 2)])
    return first, second


def coef_kernel(freq_ref, visc_ref, coef_ref):
    first, second = circulant_parts()
    freq, visc = freq_ref[0], visc_ref[0]
    half = NT // 2
    for part, sgn in enumerate((1.0, -1.0)):
        for j in range(half):
            a = 0.5 * (first[j] + sgn * first[j + half])
            b = 0.5 * (second[j] + sgn * second[j + half])
            row = part * half + j
            coef_ref[row : row + 1, :] = jnp.full((1, 128), freq * float(a) + visc * float(b), F32)


def coefficients(frequency, viscosity):
    smem = pl.BlockSpec(memory_space=pltpu.SMEM)
    return pl.pallas_call(
        coef_kernel,
        out_shape=jax.ShapeDtypeStruct((NT, 128), F32),
        in_specs=[smem, smem],
        out_specs=pl.BlockSpec(memory_space=pltpu.VMEM),
        compiler_params=pltpu.CompilerParams(vmem_limit_bytes=MIB),
        cost_estimate=pl.CostEstimate(flops=4 * 10**9, bytes_accessed=0, transcendentals=0),
        name="coefficients",
    )(frequency, viscosity)


def prep_kernel(mark_ref, s_ref, d_ref, lin_ref, elem_ref, flat, wide):
    for k, ref in enumerate((s_ref, d_ref)):
        for r in range(ROWS):
            flat[k * ROWS + r : k * ROWS + r + 1, :] = ref[0:1, r * 128 : (r + 1) * 128].astype(F32)
    flat[2 * ROWS : 256, :] = jnp.zeros((256 - 2 * ROWS, 128), F32)
    lin_ref[...] = flat[...].astype(BF16)
    half = E_DEV // 2
    low = lane_half(half)
    s = [flat[pl.ds(q, half, stride=5), :] for q in range(5)]
    d = [flat[pl.ds(ROWS + q, half, stride=5), :] for q in range(5)]
    even = [s[0], s[1], jnp.where(low, s[2], swap(d[0])), join(d[0], d[1]), join(d[1], d[2])]
    odd = [join(s[2], s[3]), join(s[3], s[4]), jnp.where(low, swap(s[4]), d[2]), d[3], d[4]]
    for q in range(5):
        wide[q, pl.ds(0, half, stride=2), :] = even[q]
        wide[q, pl.ds(1, half, stride=2), :] = odd[q]
    for q in range(5):
        elem_ref[:E_DEV, q * 128 : (q + 1) * 128] = wide[q].astype(BF16)
    elem_ref[E_DEV:, :] = jnp.zeros((SPARE, 2 * DOF), BF16)


def prep(mark, state, direction):
    vmem = pl.BlockSpec(memory_space=pltpu.VMEM)
    return pl.pallas_call(
        prep_kernel,
        out_shape=(
            jax.ShapeDtypeStruct((256, 128), BF16),
            jax.ShapeDtypeStruct((E_DEV + SPARE, 2 * DOF), BF16),
        ),
        in_specs=[pl.BlockSpec(memory_space=pl.ANY), vmem, vmem],
        out_specs=(vmem, vmem),
        scratch_shapes=[pltpu.VMEM((256, 128), F32), pltpu.VMEM((5, E_DEV, 128), F32)],
        compiler_params=pltpu.CompilerParams(vmem_limit_bytes=4 * MIB),
        name="prep",
    )(mark, state, direction)


def pair_kernel(own_ref, across_ref, pair_ref):
    pair_ref[:E_DEV, :] = own_ref[:E_DEV, :]
    pair_ref[E_DEV : 2 * E_DEV, :] = across_ref[:E_DEV, :]
    pair_ref[2 * E_DEV :, :] = jnp.zeros((SPARE, 2 * DOF), BF16)


def make_pair(own, across):
    vmem = pl.BlockSpec(memory_space=pltpu.VMEM)
    return pl.pallas_call(
        pair_kernel,
        out_shape=jax.ShapeDtypeStruct((2 * E_DEV + SPARE, 2 * DOF), BF16),
        in_specs=[vmem, vmem],
        out_specs=vmem,
        compiler_params=pltpu.CompilerParams(vmem_limit_bytes=2 * MIB),
        name="pair",
    )(own, across)


def spectral_kernel(coef_ref, x_ref, after_ref, y_ref):
    half = NT // 2
    x = x_ref[...].astype(F32).reshape(NT, 8, 128)

    def part(sgn):
        base = 0 if sgn > 0 else half
        c = [jnp.broadcast_to(coef_ref[base + j : base + j + 1, :], (8, 128)) for j in range(half)]
        u = [x[s] + sgn * x[s + half] for s in range(half)]
        out = []
        for t in range(half):
            acc = None
            for s in range(half):
                j = t - s
                term = c[j % half] * u[s]
                if acc is None:
                    acc = term
                elif j < 0 and sgn < 0:
                    acc = acc - term
                else:
                    acc = acc + term
            out.append(acc)
        return out

    even = part(1.0)
    for t in range(half):
        y_ref[t * 8 : (t + 1) * 8, :] = even[t]
    odd = part(-1.0)
    for t in range(half):
        e = y_ref[t * 8 : (t + 1) * 8, :]
        y_ref[t * 8 : (t + 1) * 8, :] = e + odd[t]
        y_ref[(t + half) * 8 : (t + half + 1) * 8, :] = e - odd[t]


def spectral_sum(coef, received, after):
    vmem = pl.BlockSpec(memory_space=pltpu.VMEM)
    return pl.pallas_call(
        spectral_kernel,
        out_shape=jax.ShapeDtypeStruct((256, 128), F32),
        in_specs=[vmem] * 2 + [pl.BlockSpec(memory_space=pl.ANY)],
        out_specs=vmem,
        compiler_params=pltpu.CompilerParams(vmem_limit_bytes=4 * MIB),
        cost_estimate=pl.CostEstimate(flops=10**11, bytes_accessed=0, transcendentals=0),
        name="spectral",
    )(coef, received, after)


def vector_tiles(elem):
    p = [elem[:, q * 128 : (q + 1) * 128] for q in range(5)]
    low = lane_half(E_DEV)
    zero = jnp.zeros((E_DEV, 128), F32)
    s = [p[0], p[1], jnp.where(low, p[2], zero), jnp.where(low, zero, swap(p[0])), join(p[0], p[1]), join(p[1], p[2])]
    d = [join(p[2], p[3]), join(p[3], p[4]), jnp.where(low, swap(p[4]), zero), jnp.where(low, zero, p[2]), p[3], p[4]]
    return s, d


def jacobian_kernel(jac_ref, elem_ref, after_ref, out_ref, weights, acc, rows):
    s, d = vector_tiles(elem_ref[:E_DEV, :].astype(F32))
    pad = jnp.zeros((128 - 2 * E_DEV, 128), F32)
    blocks = E_DEV // BLOCK
    turned = []
    for q in range(3):
        parts = []
        for b in range(blocks):
            parts += [s[q][b * BLOCK : (b + 1) * BLOCK], d[q][b * BLOCK : (b + 1) * BLOCK]]
        turned.append(jnp.concatenate(parts + [pad], axis=0).T)
    turned = jnp.concatenate(turned, axis=0)[:DOF]
    lane = lax.broadcasted_iota(jnp.int32, (DOF, 128), 1)
    for b in range(blocks):
        for i in range(4):
            at = turned if i == b else pltpu.roll(turned, (i - b) * 32 % 128, 1)
            at = jnp.where((lane >= 32 * i) & (lane < 32 * (i + 1)), at, 0.0)
            weights[b, DOF * i : DOF * (i + 1), :] = at.astype(BF16)
    e = lax.broadcasted_iota(jnp.int32, (BLOCK, 128), 0)
    keep = (lax.broadcasted_iota(jnp.int32, (BLOCK, 128), 1) & (BLOCK - 1)) == e

    def step(c, carry):
        for b in range(blocks):
            lhs = jnp.concatenate(
                [
                    jac_ref[0, b * BLOCK : (b + 1) * BLOCK, pl.ds(pl.multiple_of(c * PIECE, PIECE) + g * 4 * DOF, 4 * DOF)]
                    for g in range(GROUPS)
                ],
                axis=0,
            )
            res = jnp.dot(lhs, weights[b], preferred_element_type=F32)
            res = jnp.where(keep[None], res.reshape(GROUPS, BLOCK, 128), 0.0)
            acc[b, pl.ds(pl.multiple_of(c * GROUPS, GROUPS), GROUPS), :] = jnp.sum(res, axis=1)
        return carry

    lax.fori_loop(0, CHUNKS, step, 0)
    groups = CHUNKS * GROUPS
    lane = lax.broadcasted_iota(jnp.int32, (groups, 128), 1)
    for i in range(4):
        at = jnp.zeros((groups, 128), F32)
        for b in range(blocks):
            moved = acc[b] if i == b else pltpu.roll(acc[b], (b - i) * 32 % 128, 1)
            at = jnp.where((lane >= 32 * b) & (lane < 32 * (b + 1)), moved, at)
        rows[pl.ds(i, groups, stride=4), :] = at
    rows[DOF:, :] = jnp.zeros((384 - DOF, 128), F32)
    for q in range(3):
        back = rows[q * 128 : (q + 1) * 128, :].T
        for b in range(blocks):
            for k in range(2):
                out_ref[k * E_DEV + b * BLOCK : k * E_DEV + (b + 1) * BLOCK, q * 128 : (q + 1) * 128] = back[
                    b * 32 + k * BLOCK : b * 32 + (k + 1) * BLOCK
                ]


def jacobian_product(jacobian, elem, after):
    return pl.pallas_call(
        jacobian_kernel,
        out_shape=jax.ShapeDtypeStruct((2 * E_DEV, 384), F32),
        in_specs=[
            pl.BlockSpec(memory_space=pltpu.VMEM),
            pl.BlockSpec(memory_space=pltpu.VMEM),
            pl.BlockSpec(memory_space=pl.ANY),
        ],
        out_specs=pl.BlockSpec(memory_space=pltpu.VMEM),
        scratch_shapes=[
            pltpu.VMEM((E_DEV // BLOCK, 4 * DOF, 128), BF16),
            pltpu.VMEM((E_DEV // BLOCK, CHUNKS * GROUPS, 128), F32),
            pltpu.VMEM((384, 128), F32),
        ],
        compiler_params=pltpu.CompilerParams(vmem_limit_bytes=8 * MIB),
        cost_estimate=pl.CostEstimate(
            flops=2 * 2 * E_DEV * DOF * DOF * 48, bytes_accessed=2 * E_DEV * DOF * DOF, transcendentals=0
        ),
        name="jacobian",
    )(jacobian, elem, after)


def split(x):
    high = x.astype(BF16)
    return high, (x - high.astype(F32)).astype(BF16)


def flux_kernel(
    quad_ref, dev_ref, far_ref, near_ref, cls_ref, src_ref, time_ref, jac_ref, sel_ref, inc_ref, elem_ref, *rest
):
    tables, (res_ref, prod_ref, scratch) = rest[:-3], rest[-3:]
    me = lax.axis_index("space")
    far = far_ref[...]
    near = near_ref[...]
    cls = cls_ref[...]
    far_e = (far * 10923) >> 16
    far_l = far - far_e * 6
    near_e = (near * 10923) >> 16
    near_row = (near - near_e * 6) * E_DEV + near_e
    turn = (dev_ref[...] - me) & (N_SPACE - 1)
    block = jnp.zeros((1, SLOTS_DEV), jnp.int32)
    for at, which in enumerate((0, 4, 7, 3, 1, 5, 6, 2)):
        block = jnp.where(turn == which, at, block)
    column = block * E_DEV + far_e
    w = jnp.zeros((1, SLOTS_DEV), F32)
    for c in range(16):
        w = jnp.where(cls == c, quad_ref[:, c : c + 1], w)
    r = lax.broadcasted_iota(jnp.int32, (SLOTS_DEV, SLOTS_DEV), 0)
    c = lax.broadcasted_iota(jnp.int32, (SLOTS_DEV, SLOTS_DEV), 1)
    both = (far_l * 512 + column).astype(F32)
    code = jnp.sum(jnp.where(r == c, both, 0.0), axis=1, keepdims=True).astype(jnp.int32)
    column_s = code & 511
    far_ls = code >> 9
    total = N_SPACE * E_DEV
    pick = (lax.broadcasted_iota(jnp.int32, (SLOTS_DEV, total), 1) == column_s).astype(F32).astype(BF16)
    table = jnp.concatenate([t[: 2 * E_DEV, :] for t in tables], axis=0)
    got = jnp.dot(pick, table, preferred_element_type=F32)
    p = [got[:, q * 128 : (q + 1) * 128] for q in range(5)]
    low = lane_half(SLOTS_DEV)
    zero = jnp.zeros((SLOTS_DEV, 128), F32)
    fields = jnp.concatenate(
        [
            jnp.concatenate([p[0], p[1], jnp.where(low, p[2], zero)], axis=1),
            jnp.concatenate([join(p[2], p[3]), join(p[3], p[4]), jnp.where(low, swap(p[4]), zero)], axis=1),
        ],
        axis=0,
    ).astype(BF16)
    sel = sel_ref[...]
    faces = jnp.dot(fields, sel, preferred_element_type=F32)
    which = jnp.concatenate([far_ls, far_ls], axis=0)
    trace = jnp.zeros((2 * SLOTS_DEV, 128), F32)
    for face in range(6):
        trace = jnp.where(which == face, faces[:, face * 128 : (face + 1) * 128], trace)
    trace = jnp.concatenate([trace[:SLOTS_DEV], trace[SLOTS_DEV:]], axis=1).astype(BF16)
    rows = lax.broadcasted_iota(jnp.int32, (6 * E_DEV, SLOTS_DEV), 0)
    spread = jnp.where(rows == near_row, w, 0.0)
    high, rest_w = split(spread)
    flux = jnp.dot(high, trace, preferred_element_type=F32) + jnp.dot(rest_w, trace, preferred_element_type=F32)
    weight_sum = jnp.sum(spread, axis=1, keepdims=True)
    lhs = jnp.concatenate(
        [
            jnp.concatenate(
                [flux[f * E_DEV : (f + 1) * E_DEV, :128], flux[f * E_DEV : (f + 1) * E_DEV, 128:]], axis=0
            )
            for f in range(6)
        ],
        axis=1,
    )
    high, rest_f = split(lhs)
    dims = (((1,), (1,)), ((), ()))
    lifted = lax.dot_general(high, sel, dims, preferred_element_type=F32) + lax.dot_general(
        rest_f, sel, dims, preferred_element_type=F32
    )
    coef = jnp.zeros((E_DEV, 384), F32)
    for f in range(6):
        coef = coef + weight_sum[f * E_DEV : (f + 1) * E_DEV] * inc_ref[f : f + 1, :]
    fields_own = vector_tiles(elem_ref[:E_DEV, :].astype(F32))
    half = E_DEV // 2
    low = lane_half(half)
    for k, out_ref in enumerate((res_ref, prod_ref)):
        own = jnp.concatenate(fields_own[k][:3], axis=1)
        rows_k = slice(k * E_DEV, (k + 1) * E_DEV)
        total_k = jac_ref[rows_k, :] + coef * own - lifted[rows_k]
        for q in range(3):
            scratch[q] = total_k[:, q * 128 : (q + 1) * 128]
        even = [scratch[q, pl.ds(0, half, stride=2), :] for q in range(3)]
        odd = [scratch[q, pl.ds(1, half, stride=2), :] for q in range(3)]
        tiles = [
            even[0],
            even[1],
            jnp.where(low, even[2], swap(odd[0])),
            join(odd[0], odd[1]),
            join(odd[1], odd[2]),
        ]
        for q in range(5):
            at = time_ref[pl.ds(k * ROWS + q, half, stride=5), :] + tiles[q]
            if k == 0:
                at = src_ref[pl.ds(q, half, stride=5), :] - at
            out_ref[pl.ds(q, half, stride=5), :] = at


def finish(quad, dev, far, near, cls, source, time_terms, jac_terms, elem, tables):
    sel = np.zeros((384, 768), np.float32)
    sel[:DOF] = face_selector()
    vmem = pl.BlockSpec(memory_space=pltpu.VMEM)
    return pl.pallas_call(
        flux_kernel,
        out_shape=(jax.ShapeDtypeStruct((ROWS, 128), F32),) * 2,
        in_specs=[vmem] * (11 + len(tables)),
        out_specs=(vmem, vmem),
        scratch_shapes=[pltpu.VMEM((3, E_DEV, 128), F32)],
        compiler_params=pltpu.CompilerParams(vmem_limit_bytes=12 * MIB),
        name="finish",
    )(
        quad.reshape(1, 16), dev, far, near, cls, source, time_terms, jac_terms,
        jnp.asarray(sel, BF16), jnp.asarray(face_incidence()), elem, *tables,
    )


def per_device(
    harmonic_state,
    direction,
    source,
    jacobian,
    frequency,
    viscosity,
    quad_weight,
    partner_device,
    partner_face,
    local_face,
    weight_index,
):
    coef = coefficients(frequency, viscosity)
    lin, elem = prep(coef, harmonic_state, direction)

    def over_space(x, turn):
        return lax.ppermute(x, "space", [(i, (i + turn) % N_SPACE) for i in range(N_SPACE)])

    across = over_space(elem, 4)
    received = lax.all_to_all(lin, "inst", 0, 0, tiled=True)
    pair = make_pair(elem, across)
    others = [over_space(pair, turn) for turn in (1, -1, 2)]
    back = spectral_sum(coef, received, pair)
    time_terms = lax.all_to_all(back, "inst", 0, 0, tiled=True)
    jac_terms = jacobian_product(jacobian, elem, back)
    residual, product = finish(
        quad_weight,
        partner_device.reshape(1, SLOTS_DEV),
        partner_face,
        local_face,
        weight_index,
        source.reshape(ROWS, 128),
        time_terms,
        jac_terms,
        elem,
        [pair] + others,
    )
    return residual.reshape(1, FLAT), product.reshape(1, FLAT)


def solution(mesh):
    in_specs = (
        P("inst", "space"),
        P("inst", "space"),
        P("inst", "space"),
        P("inst", "space", None),
        P(),
        P(),
        P(),
        P("inst", "space", None),
        P("inst", "space"),
        P("inst", "space"),
        P("inst", "space"),
    )
    out_specs = (P("inst", "space"), P("inst", "space"))
    return jax.shard_map(
        per_device, mesh=mesh, in_specs=in_specs, out_specs=out_specs, check_vma=False
    )
```

```python
import jax
import jax.numpy as jnp
import numpy as np
from jax import lax
from jax.experimental import pallas as pl
from jax.experimental.pallas import tpu as pltpu
from jax.sharding import PartitionSpec as P

VARS = 5
PNODE = 4
E_DEV = 48
DOF = 320
SLOTS_DEV = 192
N_SPACE = 8
NT = 32
FLAT = E_DEV * DOF
ROWS = FLAT // 128
CHUNKS = 5
GROUPS = 16
BLOCK = 16
PIECE = GROUPS * 4 * DOF
SPARE = 16
MIB = 1024 * 1024
F32 = jnp.float32
BF16 = jnp.bfloat16


def face_selector():
    table = np.zeros((DOF, 6 * 128), np.float32)
    for face in range(6):
        fixed = 0 if face % 2 == 0 else PNODE - 1
        for comp in range(VARS):
            for first in range(PNODE):
                for second in range(PNODE):
                    if face < 2:
                        i, j, k = fixed, first, second
                    elif face < 4:
                        i, j, k = first, fixed, second
                    else:
                        i, j, k = first, second, fixed
                    table[comp * 64 + i * 16 + j * 4 + k, face * 128 + comp * 16 + first * 4 + second] = 1.0
    return table


def face_incidence():
    rows = np.zeros((8, 384), np.float32)
    for face in range(6):
        rows[face, :DOF] = face_selector()[:, face * 128 : (face + 1) * 128].sum(axis=1)
    return rows


def lane_half(rows):
    return lax.broadcasted_iota(jnp.int32, (rows, 128), 1) < 64


def swap(x):
    return pltpu.roll(x, 64, 1)


def join(low, high):
    return jnp.where(lane_half(low.shape[0]), swap(low), swap(high))


def circulant_parts():
    j = np.arange(1, NT)
    sign = 1.0 - 2.0 * (j % 2)
    angle = np.pi * j / NT
    first = np.concatenate([[0.0], 0.5 * sign * np.cos(angle) / np.sin(angle)])
    second = np.concatenate([[-(NT * NT + 2) / 12.0], -sign / (2.0 * np.sin(angle) ** 2)])
    return first, second


def coef_kernel(freq_ref, visc_ref, coef_ref):
    first, second = circulant_parts()
    freq, visc = freq_ref[0], visc_ref[0]
    half = NT // 2
    for part, sgn in enumerate((1.0, -1.0)):
        for j in range(half):
            a = 0.5 * (first[j] + sgn * first[j + half])
            b = 0.5 * (second[j] + sgn * second[j + half])
            row = part * half + j
            coef_ref[row : row + 1, :] = jnp.full((1, 128), freq * float(a) + visc * float(b), F32)


def coefficients(frequency, viscosity):
    smem = pl.BlockSpec(memory_space=pltpu.SMEM)
    return pl.pallas_call(
        coef_kernel,
        out_shape=jax.ShapeDtypeStruct((NT, 128), F32),
        in_specs=[smem, smem],
        out_specs=pl.BlockSpec(memory_space=pltpu.VMEM),
        compiler_params=pltpu.CompilerParams(vmem_limit_bytes=MIB),
        cost_estimate=pl.CostEstimate(flops=4 * 10**9, bytes_accessed=0, transcendentals=0),
        name="coefficients",
    )(frequency, viscosity)


def prep_kernel(mark_ref, s_ref, d_ref, lin_ref, elem_ref, flat, wide):
    for k, ref in enumerate((s_ref, d_ref)):
        for r in range(ROWS):
            flat[k * ROWS + r : k * ROWS + r + 1, :] = ref[0:1, r * 128 : (r + 1) * 128].astype(F32)
    flat[2 * ROWS : 256, :] = jnp.zeros((256 - 2 * ROWS, 128), F32)
    lin_ref[...] = flat[...].astype(BF16)
    half = E_DEV // 2
    low = lane_half(half)
    s = [flat[pl.ds(q, half, stride=5), :] for q in range(5)]
    d = [flat[pl.ds(ROWS + q, half, stride=5), :] for q in range(5)]
    even = [s[0], s[1], jnp.where(low, s[2], swap(d[0])), join(d[0], d[1]), join(d[1], d[2])]
    odd = [join(s[2], s[3]), join(s[3], s[4]), jnp.where(low, swap(s[4]), d[2]), d[3], d[4]]
    for q in range(5):
        wide[q, pl.ds(0, half, stride=2), :] = even[q]
        wide[q, pl.ds(1, half, stride=2), :] = odd[q]
    for q in range(5):
        elem_ref[:E_DEV, q * 128 : (q + 1) * 128] = wide[q].astype(BF16)
    elem_ref[E_DEV:, :] = jnp.zeros((SPARE // 2, 2 * DOF), BF16)


def prep(mark, state, direction):
    vmem = pl.BlockSpec(memory_space=pltpu.VMEM)
    return pl.pallas_call(
        prep_kernel,
        out_shape=(
            jax.ShapeDtypeStruct((256, 128), BF16),
            jax.ShapeDtypeStruct((E_DEV + SPARE // 2, 2 * DOF), BF16),
        ),
        in_specs=[pl.BlockSpec(memory_space=pl.ANY), vmem, vmem],
        out_specs=(vmem, vmem),
        scratch_shapes=[pltpu.VMEM((256, 128), F32), pltpu.VMEM((5, E_DEV, 128), F32)],
        compiler_params=pltpu.CompilerParams(vmem_limit_bytes=4 * MIB),
        name="prep",
    )(mark, state, direction)


def pair_kernel(own_ref, across_ref, pair_ref):
    pair_ref[:E_DEV, :] = own_ref[:E_DEV, :]
    pair_ref[E_DEV : 2 * E_DEV, :] = across_ref[:E_DEV, :]
    pair_ref[2 * E_DEV :, :] = jnp.zeros((SPARE, 2 * DOF), BF16)


def make_pair(own, across):
    vmem = pl.BlockSpec(memory_space=pltpu.VMEM)
    return pl.pallas_call(
        pair_kernel,
        out_shape=jax.ShapeDtypeStruct((2 * E_DEV + SPARE, 2 * DOF), BF16),
        in_specs=[vmem, vmem],
        out_specs=vmem,
        compiler_params=pltpu.CompilerParams(vmem_limit_bytes=2 * MIB),
        name="pair",
    )(own, across)


def spectral_kernel(coef_ref, x_ref, after_ref, y_ref):
    half = NT // 2
    x = x_ref[...].astype(F32).reshape(NT, 8, 128)

    def part(sgn):
        base = 0 if sgn > 0 else half
        c = [jnp.broadcast_to(coef_ref[base + j : base + j + 1, :], (8, 128)) for j in range(half)]
        u = [x[s] + sgn * x[s + half] for s in range(half)]
        out = []
        for t in range(half):
            acc = None
            for s in range(half):
                j = t - s
                term = c[j % half] * u[s]
                if acc is None:
                    acc = term
                elif j < 0 and sgn < 0:
                    acc = acc - term
                else:
                    acc = acc + term
            out.append(acc)
        return out

    even = part(1.0)
    for t in range(half):
        y_ref[t * 8 : (t + 1) * 8, :] = even[t]
    odd = part(-1.0)
    for t in range(half):
        e = y_ref[t * 8 : (t + 1) * 8, :]
        y_ref[t * 8 : (t + 1) * 8, :] = e + odd[t]
        y_ref[(t + half) * 8 : (t + half + 1) * 8, :] = e - odd[t]


def spectral_sum(coef, received, after):
    vmem = pl.BlockSpec(memory_space=pltpu.VMEM)
    return pl.pallas_call(
        spectral_kernel,
        out_shape=jax.ShapeDtypeStruct((256, 128), F32),
        in_specs=[vmem] * 2 + [pl.BlockSpec(memory_space=pl.ANY)],
        out_specs=vmem,
        compiler_params=pltpu.CompilerParams(vmem_limit_bytes=4 * MIB),
        cost_estimate=pl.CostEstimate(flops=10**10, bytes_accessed=0, transcendentals=0),
        name="spectral",
    )(coef, received, after)


def vector_tiles(elem):
    p = [elem[:, q * 128 : (q + 1) * 128] for q in range(5)]
    low = lane_half(E_DEV)
    zero = jnp.zeros((E_DEV, 128), F32)
    s = [p[0], p[1], jnp.where(low, p[2], zero), jnp.where(low, zero, swap(p[0])), join(p[0], p[1]), join(p[1], p[2])]
    d = [join(p[2], p[3]), join(p[3], p[4]), jnp.where(low, swap(p[4]), zero), jnp.where(low, zero, p[2]), p[3], p[4]]
    return s, d


def jacobian_kernel(jac_hbm, elem_ref, after_ref, out_ref, held, weights, acc, rows, sems):
    def piece(c, start):
        return pltpu.make_async_copy(jac_hbm.at[0, :, pl.ds(start, PIECE)], held.at[c], sems.at[c])

    for c in range(CHUNKS):
        piece(c, c * PIECE).start()
    s, d = vector_tiles(elem_ref[:E_DEV, :].astype(F32))
    pad = jnp.zeros((128 - 2 * E_DEV, 128), F32)
    blocks = E_DEV // BLOCK
    turned = []
    for q in range(3):
        parts = []
        for b in range(blocks):
            parts += [s[q][b * BLOCK : (b + 1) * BLOCK], d[q][b * BLOCK : (b + 1) * BLOCK]]
        turned.append(jnp.concatenate(parts + [pad], axis=0).T)
    turned = jnp.concatenate(turned, axis=0)[:DOF]
    lane = lax.broadcasted_iota(jnp.int32, (DOF, 128), 1)
    for b in range(blocks):
        for i in range(4):
            at = turned if i == b else pltpu.roll(turned, (i - b) * 32 % 128, 1)
            at = jnp.where((lane >= 32 * i) & (lane < 32 * (i + 1)), at, 0.0)
            weights[b, DOF * i : DOF * (i + 1), :] = at.astype(BF16)
    e = lax.broadcasted_iota(jnp.int32, (BLOCK, 128), 0)
    keep = (lax.broadcasted_iota(jnp.int32, (BLOCK, 128), 1) & (BLOCK - 1)) == e

    def step(c, carry):
        piece(c, pl.multiple_of(c * PIECE, PIECE)).wait()
        for b in range(blocks):
            lhs = jnp.concatenate(
                [
                    held[c, b * BLOCK : (b + 1) * BLOCK, g * 4 * DOF : (g + 1) * 4 * DOF]
                    for g in range(GROUPS)
                ],
                axis=0,
            )
            res = jnp.dot(lhs, weights[b], preferred_element_type=F32)
            res = jnp.where(keep[None], res.reshape(GROUPS, BLOCK, 128), 0.0)
            acc[b, pl.ds(pl.multiple_of(c * GROUPS, GROUPS), GROUPS), :] = jnp.sum(res, axis=1)
        return carry

    lax.fori_loop(0, CHUNKS, step, 0)
    groups = CHUNKS * GROUPS
    lane = lax.broadcasted_iota(jnp.int32, (groups, 128), 1)
    for i in range(4):
        at = jnp.zeros((groups, 128), F32)
        for b in range(blocks):
            moved = acc[b] if i == b else pltpu.roll(acc[b], (b - i) * 32 % 128, 1)
            at = jnp.where((lane >= 32 * b) & (lane < 32 * (b + 1)), moved, at)
        rows[pl.ds(i, groups, stride=4), :] = at
    rows[DOF:, :] = jnp.zeros((384 - DOF, 128), F32)
    for q in range(3):
        back = rows[q * 128 : (q + 1) * 128, :].T
        for b in range(blocks):
            for k in range(2):
                out_ref[k * E_DEV + b * BLOCK : k * E_DEV + (b + 1) * BLOCK, q * 128 : (q + 1) * 128] = back[
                    b * 32 + k * BLOCK : b * 32 + (k + 1) * BLOCK
                ]


def jacobian_product(jacobian, elem, after):
    return pl.pallas_call(
        jacobian_kernel,
        out_shape=jax.ShapeDtypeStruct((2 * E_DEV, 384), F32),
        in_specs=[
            pl.BlockSpec(memory_space=pltpu.HBM),
            pl.BlockSpec(memory_space=pltpu.VMEM),
            pl.BlockSpec(memory_space=pl.ANY),
        ],
        out_specs=pl.BlockSpec(memory_space=pltpu.VMEM),
        scratch_shapes=[
            pltpu.VMEM((CHUNKS, E_DEV, PIECE), BF16),
            pltpu.VMEM((E_DEV // BLOCK, 4 * DOF, 128), BF16),
            pltpu.VMEM((E_DEV // BLOCK, CHUNKS * GROUPS, 128), F32),
            pltpu.VMEM((384, 128), F32),
            pltpu.SemaphoreType.DMA((CHUNKS,)),
        ],
        compiler_params=pltpu.CompilerParams(vmem_limit_bytes=49 * MIB),
        cost_estimate=pl.CostEstimate(
            flops=2 * 2 * E_DEV * DOF * DOF * 48, bytes_accessed=2 * E_DEV * DOF * DOF, transcendentals=0
        ),
        name="jacobian",
    )(jacobian, elem, after)


def split(x):
    high = x.astype(BF16)
    return high, (x - high.astype(F32)).astype(BF16)


def flux_kernel(
    quad_ref, dev_ref, far_ref, near_ref, cls_ref, src_ref, time_ref, jac_ref, sel_ref, lift_ref, inc_ref, elem_ref, *rest
):
    tables, (res_ref, prod_ref, scratch) = rest[:-3], rest[-3:]
    me = lax.axis_index("space")
    far = far_ref[...]
    near = near_ref[...]
    cls = cls_ref[...]
    far_e = (far * 10923) >> 16
    far_l = far - far_e * 6
    near_e = (near * 10923) >> 16
    near_row = (near - near_e * 6) * E_DEV + near_e
    turn = (dev_ref[...] - me) & (N_SPACE - 1)
    block = jnp.zeros((1, SLOTS_DEV), jnp.int32)
    for at, which in enumerate((0, 4, 7, 3, 1, 5, 6, 2)):
        block = jnp.where(turn == which, at, block)
    column = block * E_DEV + far_e
    w = jnp.zeros((1, SLOTS_DEV), F32)
    for c in range(16):
        w = jnp.where(cls == c, quad_ref[:, c : c + 1], w)
    r = lax.broadcasted_iota(jnp.int32, (SLOTS_DEV, SLOTS_DEV), 0)
    c = lax.broadcasted_iota(jnp.int32, (SLOTS_DEV, SLOTS_DEV), 1)
    both = (far_l * 512 + column).astype(F32)
    code = jnp.sum(jnp.where(r == c, both, 0.0), axis=1, keepdims=True).astype(jnp.int32)
    column_s = code & 511
    far_ls = code >> 9
    total = N_SPACE * E_DEV
    pick = (lax.broadcasted_iota(jnp.int32, (SLOTS_DEV, total), 1) == column_s).astype(F32).astype(BF16)
    table = jnp.concatenate([t[: 2 * E_DEV, :] for t in tables], axis=0)
    got = jnp.dot(pick, table, preferred_element_type=F32)
    p = [got[:, q * 128 : (q + 1) * 128] for q in range(5)]
    low = lane_half(SLOTS_DEV)
    zero = jnp.zeros((SLOTS_DEV, 128), F32)
    fields = jnp.concatenate(
        [
            jnp.concatenate([p[0], p[1], jnp.where(low, p[2], zero)], axis=1),
            jnp.concatenate([join(p[2], p[3]), join(p[3], p[4]), jnp.where(low, swap(p[4]), zero)], axis=1),
        ],
        axis=0,
    ).astype(BF16)
    faces = jnp.dot(fields, sel_ref[...], preferred_element_type=F32)
    which = jnp.concatenate([far_ls, far_ls], axis=0)
    trace = jnp.zeros((2 * SLOTS_DEV, 128), F32)
    for face in range(6):
        trace = jnp.where(which == face, faces[:, face * 128 : (face + 1) * 128], trace)
    trace = jnp.concatenate([trace[:SLOTS_DEV], trace[SLOTS_DEV:]], axis=1).astype(BF16)
    rows = lax.broadcasted_iota(jnp.int32, (6 * E_DEV, SLOTS_DEV), 0)
    spread = jnp.where(rows == near_row, w, 0.0)
    flux = jnp.dot(jnp.concatenate(split(spread), axis=0), trace, preferred_element_type=F32)
    flux = flux[: 6 * E_DEV] + flux[6 * E_DEV :]
    weight_sum = jnp.sum(spread, axis=1, keepdims=True)
    lhs = jnp.concatenate(
        [
            jnp.concatenate(
                [flux[f * E_DEV : (f + 1) * E_DEV, :128], flux[f * E_DEV : (f + 1) * E_DEV, 128:]], axis=0
            )
            for f in range(6)
        ],
        axis=1,
    )
    lifted = jnp.dot(jnp.concatenate(split(lhs), axis=0), lift_ref[...], preferred_element_type=F32)
    lifted = lifted[: 2 * E_DEV] + lifted[2 * E_DEV :]
    coef = jnp.zeros((E_DEV, 384), F32)
    for f in range(6):
        coef = coef + weight_sum[f * E_DEV : (f + 1) * E_DEV] * inc_ref[f : f + 1, :]
    fields_own = vector_tiles(elem_ref[:E_DEV, :].astype(F32))
    half = E_DEV // 2
    low = lane_half(half)
    for k, out_ref in enumerate((res_ref, prod_ref)):
        own = jnp.concatenate(fields_own[k][:3], axis=1)
        rows_k = slice(k * E_DEV, (k + 1) * E_DEV)
        total_k = jac_ref[rows_k, :] + coef * own - lifted[rows_k]
        for q in range(3):
            scratch[q] = total_k[:, q * 128 : (q + 1) * 128]
        even = [scratch[q, pl.ds(0, half, stride=2), :] for q in range(3)]
        odd = [scratch[q, pl.ds(1, half, stride=2), :] for q in range(3)]
        tiles = [
            even[0],
            even[1],
            jnp.where(low, even[2], swap(odd[0])),
            join(odd[0], odd[1]),
            join(odd[1], odd[2]),
        ]
        for q in range(5):
            at = time_ref[pl.ds(k * ROWS + q, half, stride=5), :] + tiles[q]
            if k == 0:
                at = src_ref[pl.ds(q, half, stride=5), :] - at
            out_ref[pl.ds(q, half, stride=5), :] = at


def finish(quad, dev, far, near, cls, source, time_terms, jac_terms, elem, tables):
    sel = np.zeros((384, 768), np.float32)
    sel[:DOF] = face_selector()
    vmem = pl.BlockSpec(memory_space=pltpu.VMEM)
    return pl.pallas_call(
        flux_kernel,
        out_shape=(jax.ShapeDtypeStruct((ROWS, 128), F32),) * 2,
        in_specs=[vmem] * (12 + len(tables)),
        out_specs=(vmem, vmem),
        scratch_shapes=[pltpu.VMEM((3, E_DEV, 128), F32)],
        compiler_params=pltpu.CompilerParams(vmem_limit_bytes=12 * MIB),
        name="finish",
    )(
        quad.reshape(1, 16), dev, far, near, cls, source, time_terms, jac_terms,
        jnp.asarray(sel, BF16), jnp.asarray(sel.T, BF16), jnp.asarray(face_incidence()), elem, *tables,
    )


def per_device(
    harmonic_state,
    direction,
    source,
    jacobian,
    frequency,
    viscosity,
    quad_weight,
    partner_device,
    partner_face,
    local_face,
    weight_index,
):
    coef = coefficients(frequency, viscosity)
    lin, elem = prep(coef, harmonic_state, direction)

    def over_space(x, turn):
        return lax.ppermute(x, "space", [(i, (i + turn) % N_SPACE) for i in range(N_SPACE)])

    across = over_space(elem, 4)
    received = lax.all_to_all(lin, "inst", 0, 0, tiled=True)
    pair = make_pair(elem, across)
    others = [over_space(pair, turn) for turn in (1, -1, 2)]
    back = spectral_sum(coef, received, pair)
    time_terms = lax.all_to_all(back, "inst", 0, 0, tiled=True)
    jac_terms = jacobian_product(jacobian, elem, back)
    residual, product = finish(
        quad_weight,
        partner_device.reshape(1, SLOTS_DEV),
        partner_face,
        local_face,
        weight_index,
        source.reshape(ROWS, 128),
        time_terms,
        jac_terms,
        elem,
        [pair] + others,
    )
    return residual.reshape(1, FLAT), product.reshape(1, FLAT)


def solution(mesh):
    in_specs = (
        P("inst", "space"),
        P("inst", "space"),
        P("inst", "space"),
        P("inst", "space", None),
        P(),
        P(),
        P(),
        P("inst", "space", None),
        P("inst", "space"),
        P("inst", "space"),
        P("inst", "space"),
    )
    out_specs = (P("inst", "space"), P("inst", "space"))
    return jax.shard_map(
        per_device, mesh=mesh, in_specs=in_specs, out_specs=out_specs, check_vma=False
    )
```

```python
import jax
import jax.numpy as jnp
import numpy as np
from jax import lax
from jax.experimental import pallas as pl
from jax.experimental.pallas import tpu as pltpu
from jax.sharding import PartitionSpec as P

VARS = 5
PNODE = 4
E_DEV = 48
DOF = 320
SLOTS_DEV = 192
N_SPACE = 8
NT = 32
FLAT = E_DEV * DOF
ROWS = FLAT // 128
CHUNKS = 5
GROUPS = 16
BLOCK = 16
PIECE = GROUPS * 4 * DOF
SPARE = 16
MIB = 1024 * 1024
F32 = jnp.float32
BF16 = jnp.bfloat16


def face_selector():
    table = np.zeros((DOF, 6 * 128), np.float32)
    for face in range(6):
        fixed = 0 if face % 2 == 0 else PNODE - 1
        for comp in range(VARS):
            for first in range(PNODE):
                for second in range(PNODE):
                    if face < 2:
                        i, j, k = fixed, first, second
                    elif face < 4:
                        i, j, k = first, fixed, second
                    else:
                        i, j, k = first, second, fixed
                    table[comp * 64 + i * 16 + j * 4 + k, face * 128 + comp * 16 + first * 4 + second] = 1.0
    return table


def face_incidence():
    rows = np.zeros((8, 384), np.float32)
    for face in range(6):
        rows[face, :DOF] = face_selector()[:, face * 128 : (face + 1) * 128].sum(axis=1)
    return rows


def lane_half(rows):
    return lax.broadcasted_iota(jnp.int32, (rows, 128), 1) < 64


def swap(x):
    return pltpu.roll(x, 64, 1)


def join(low, high):
    return jnp.where(lane_half(low.shape[0]), swap(low), swap(high))


def circulant_parts():
    j = np.arange(1, NT)
    sign = 1.0 - 2.0 * (j % 2)
    angle = np.pi * j / NT
    first = np.concatenate([[0.0], 0.5 * sign * np.cos(angle) / np.sin(angle)])
    second = np.concatenate([[-(NT * NT + 2) / 12.0], -sign / (2.0 * np.sin(angle) ** 2)])
    return first, second


def coef_kernel(freq_ref, visc_ref, coef_ref):
    first, second = circulant_parts()
    freq, visc = freq_ref[0], visc_ref[0]
    half = NT // 2
    for part, sgn in enumerate((1.0, -1.0)):
        for j in range(half):
            a = 0.5 * (first[j] + sgn * first[j + half])
            b = 0.5 * (second[j] + sgn * second[j + half])
            row = part * half + j
            coef_ref[row : row + 1, :] = jnp.full((1, 128), freq * float(a) + visc * float(b), F32)


def coefficients(frequency, viscosity):
    smem = pl.BlockSpec(memory_space=pltpu.SMEM)
    return pl.pallas_call(
        coef_kernel,
        out_shape=jax.ShapeDtypeStruct((NT, 128), F32),
        in_specs=[smem, smem],
        out_specs=pl.BlockSpec(memory_space=pltpu.VMEM),
        compiler_params=pltpu.CompilerParams(vmem_limit_bytes=MIB),
        cost_estimate=pl.CostEstimate(flops=4 * 10**9, bytes_accessed=0, transcendentals=0),
        name="coefficients",
    )(frequency, viscosity)


def prep_kernel(mark_ref, s_ref, d_ref, lin_ref, elem_ref, flat, wide):
    for k, ref in enumerate((s_ref, d_ref)):
        for r in range(ROWS):
            flat[k * ROWS + r : k * ROWS + r + 1, :] = ref[0:1, r * 128 : (r + 1) * 128].astype(F32)
    flat[2 * ROWS : 256, :] = jnp.zeros((256 - 2 * ROWS, 128), F32)
    lin_ref[...] = flat[...].astype(BF16)
    half = E_DEV // 2
    low = lane_half(half)
    s = [flat[pl.ds(q, half, stride=5), :] for q in range(5)]
    d = [flat[pl.ds(ROWS + q, half, stride=5), :] for q in range(5)]
    even = [s[0], s[1], jnp.where(low, s[2], swap(d[0])), join(d[0], d[1]), join(d[1], d[2])]
    odd = [join(s[2], s[3]), join(s[3], s[4]), jnp.where(low, swap(s[4]), d[2]), d[3], d[4]]
    for q in range(5):
        wide[q, pl.ds(0, half, stride=2), :] = even[q]
        wide[q, pl.ds(1, half, stride=2), :] = odd[q]
    for q in range(5):
        elem_ref[:E_DEV, q * 128 : (q + 1) * 128] = wide[q].astype(BF16)
    elem_ref[E_DEV:, :] = jnp.zeros((SPARE // 2, 2 * DOF), BF16)


def prep(mark, state, direction):
    vmem = pl.BlockSpec(memory_space=pltpu.VMEM)
    return pl.pallas_call(
        prep_kernel,
        out_shape=(
            jax.ShapeDtypeStruct((256, 128), BF16),
            jax.ShapeDtypeStruct((E_DEV + SPARE // 2, 2 * DOF), BF16),
        ),
        in_specs=[pl.BlockSpec(memory_space=pl.ANY), vmem, vmem],
        out_specs=(vmem, vmem),
        scratch_shapes=[pltpu.VMEM((256, 128), F32), pltpu.VMEM((5, E_DEV, 128), F32)],
        compiler_params=pltpu.CompilerParams(vmem_limit_bytes=4 * MIB),
        name="prep",
    )(mark, state, direction)


def pair_kernel(own_ref, across_ref, pair_ref):
    pair_ref[:E_DEV, :] = own_ref[:E_DEV, :]
    pair_ref[E_DEV : 2 * E_DEV, :] = across_ref[:E_DEV, :]
    pair_ref[2 * E_DEV :, :] = jnp.zeros((SPARE, 2 * DOF), BF16)


def make_pair(own, across):
    vmem = pl.BlockSpec(memory_space=pltpu.VMEM)
    return pl.pallas_call(
        pair_kernel,
        out_shape=jax.ShapeDtypeStruct((2 * E_DEV + SPARE, 2 * DOF), BF16),
        in_specs=[vmem, vmem],
        out_specs=vmem,
        compiler_params=pltpu.CompilerParams(vmem_limit_bytes=2 * MIB),
        name="pair",
    )(own, across)


def spectral_kernel(coef_ref, x_ref, after_ref, y_ref):
    half = NT // 2
    x = x_ref[...].astype(F32).reshape(NT, 8, 128)

    def part(sgn):
        base = 0 if sgn > 0 else half
        c = [jnp.broadcast_to(coef_ref[base + j : base + j + 1, :], (8, 128)) for j in range(half)]
        u = [x[s] + sgn * x[s + half] for s in range(half)]
        out = []
        for t in range(half):
            acc = None
            for s in range(half):
                j = t - s
                term = c[j % half] * u[s]
                if acc is None:
                    acc = term
                elif j < 0 and sgn < 0:
                    acc = acc - term
                else:
                    acc = acc + term
            out.append(acc)
        return out

    even = part(1.0)
    for t in range(half):
        y_ref[t * 8 : (t + 1) * 8, :] = even[t]
    odd = part(-1.0)
    for t in range(half):
        e = y_ref[t * 8 : (t + 1) * 8, :]
        y_ref[t * 8 : (t + 1) * 8, :] = e + odd[t]
        y_ref[(t + half) * 8 : (t + half + 1) * 8, :] = e - odd[t]


def spectral_sum(coef, received, after):
    vmem = pl.BlockSpec(memory_space=pltpu.VMEM)
    return pl.pallas_call(
        spectral_kernel,
        out_shape=jax.ShapeDtypeStruct((256, 128), F32),
        in_specs=[vmem] * 2 + [pl.BlockSpec(memory_space=pl.ANY)],
        out_specs=vmem,
        compiler_params=pltpu.CompilerParams(vmem_limit_bytes=4 * MIB),
        cost_estimate=pl.CostEstimate(flops=10**10, bytes_accessed=0, transcendentals=0),
        name="spectral",
    )(coef, received, after)


def vector_tiles(elem):
    p = [elem[:, q * 128 : (q + 1) * 128] for q in range(5)]
    low = lane_half(E_DEV)
    zero = jnp.zeros((E_DEV, 128), F32)
    s = [p[0], p[1], jnp.where(low, p[2], zero), jnp.where(low, zero, swap(p[0])), join(p[0], p[1]), join(p[1], p[2])]
    d = [join(p[2], p[3]), join(p[3], p[4]), jnp.where(low, swap(p[4]), zero), jnp.where(low, zero, p[2]), p[3], p[4]]
    return s, d


def jacobian_kernel(jac_hbm, elem_ref, after_ref, out_ref, held, weights, acc, rows, sems):
    def piece(c, start):
        return pltpu.make_async_copy(jac_hbm.at[0, :, pl.ds(start, PIECE)], held.at[c], sems.at[c])

    for c in range(CHUNKS):
        piece(c, c * PIECE).start()
    s, d = vector_tiles(elem_ref[:E_DEV, :].astype(F32))
    pad = jnp.zeros((128 - 2 * E_DEV, 128), F32)
    blocks = E_DEV // BLOCK
    turned = []
    for q in range(3):
        parts = []
        for b in range(blocks):
            parts += [s[q][b * BLOCK : (b + 1) * BLOCK], d[q][b * BLOCK : (b + 1) * BLOCK]]
        turned.append(jnp.concatenate(parts + [pad], axis=0).T)
    turned = jnp.concatenate(turned, axis=0)[:DOF]
    lane = lax.broadcasted_iota(jnp.int32, (DOF, 128), 1)
    for b in range(blocks):
        for i in range(4):
            at = turned if i == b else pltpu.roll(turned, (i - b) * 32 % 128, 1)
            at = jnp.where((lane >= 32 * i) & (lane < 32 * (i + 1)), at, 0.0)
            weights[b, DOF * i : DOF * (i + 1), :] = at.astype(BF16)
    e = lax.broadcasted_iota(jnp.int32, (BLOCK, 128), 0)
    keep = (lax.broadcasted_iota(jnp.int32, (BLOCK, 128), 1) & (BLOCK - 1)) == e

    def step(c, carry):
        piece(c, pl.multiple_of(c * PIECE, PIECE)).wait()
        for b in range(blocks):
            lhs = jnp.concatenate(
                [
                    held[c, b * BLOCK : (b + 1) * BLOCK, g * 4 * DOF : (g + 1) * 4 * DOF]
                    for g in range(GROUPS)
                ],
                axis=0,
            )
            res = jnp.dot(lhs, weights[b], preferred_element_type=F32)
            res = jnp.where(keep[None], res.reshape(GROUPS, BLOCK, 128), 0.0)
            acc[b, pl.ds(pl.multiple_of(c * GROUPS, GROUPS), GROUPS), :] = jnp.sum(res, axis=1)
        return carry

    lax.fori_loop(0, CHUNKS, step, 0)
    groups = CHUNKS * GROUPS
    lane = lax.broadcasted_iota(jnp.int32, (groups, 128), 1)
    for i in range(4):
        at = jnp.zeros((groups, 128), F32)
        for b in range(blocks):
            moved = acc[b] if i == b else pltpu.roll(acc[b], (b - i) * 32 % 128, 1)
            at = jnp.where((lane >= 32 * b) & (lane < 32 * (b + 1)), moved, at)
        rows[pl.ds(i, groups, stride=4), :] = at
    rows[DOF:, :] = jnp.zeros((384 - DOF, 128), F32)
    for q in range(3):
        back = rows[q * 128 : (q + 1) * 128, :].T
        for b in range(blocks):
            for k in range(2):
                out_ref[k * E_DEV + b * BLOCK : k * E_DEV + (b + 1) * BLOCK, q * 128 : (q + 1) * 128] = back[
                    b * 32 + k * BLOCK : b * 32 + (k + 1) * BLOCK
                ]


def jacobian_product(jacobian, elem, after):
    return pl.pallas_call(
        jacobian_kernel,
        out_shape=jax.ShapeDtypeStruct((2 * E_DEV, 384), F32),
        in_specs=[
            pl.BlockSpec(memory_space=pltpu.HBM),
            pl.BlockSpec(memory_space=pltpu.VMEM),
            pl.BlockSpec(memory_space=pl.ANY),
        ],
        out_specs=pl.BlockSpec(memory_space=pltpu.VMEM),
        scratch_shapes=[
            pltpu.VMEM((CHUNKS, E_DEV, PIECE), BF16),
            pltpu.VMEM((E_DEV // BLOCK, 4 * DOF, 128), BF16),
            pltpu.VMEM((E_DEV // BLOCK, CHUNKS * GROUPS, 128), F32),
            pltpu.VMEM((384, 128), F32),
            pltpu.SemaphoreType.DMA((CHUNKS,)),
        ],
        compiler_params=pltpu.CompilerParams(vmem_limit_bytes=49 * MIB),
        cost_estimate=pl.CostEstimate(
            flops=2 * 2 * E_DEV * DOF * DOF * 48, bytes_accessed=2 * E_DEV * DOF * DOF, transcendentals=0
        ),
        name="jacobian",
    )(jacobian, elem, after)


def split(x):
    high = x.astype(BF16)
    return high, (x - high.astype(F32)).astype(BF16)


def flux_kernel(
    quad_ref, dev_ref, far_ref, near_ref, cls_ref, jac_ref, sel_ref, lift_ref, inc_ref, elem_ref, *rest
):
    tables, out_ref = rest[:-1], rest[-1]
    me = lax.axis_index("space")
    far = far_ref[...]
    near = near_ref[...]
    cls = cls_ref[...]
    far_e = (far * 10923) >> 16
    far_l = far - far_e * 6
    near_e = (near * 10923) >> 16
    near_row = (near - near_e * 6) * E_DEV + near_e
    turn = (dev_ref[...] - me) & (N_SPACE - 1)
    block = jnp.zeros((1, SLOTS_DEV), jnp.int32)
    for at, which in enumerate((0, 4, 7, 3, 1, 5, 6, 2)):
        block = jnp.where(turn == which, at, block)
    column = block * E_DEV + far_e
    w = jnp.zeros((1, SLOTS_DEV), F32)
    for c in range(16):
        w = jnp.where(cls == c, quad_ref[:, c : c + 1], w)
    r = lax.broadcasted_iota(jnp.int32, (SLOTS_DEV, SLOTS_DEV), 0)
    c = lax.broadcasted_iota(jnp.int32, (SLOTS_DEV, SLOTS_DEV), 1)
    both = (far_l * 512 + column).astype(F32)
    code = jnp.sum(jnp.where(r == c, both, 0.0), axis=1, keepdims=True).astype(jnp.int32)
    column_s = code & 511
    far_ls = code >> 9
    total = N_SPACE * E_DEV
    pick = (lax.broadcasted_iota(jnp.int32, (SLOTS_DEV, total), 1) == column_s).astype(F32).astype(BF16)
    table = jnp.concatenate([t[: 2 * E_DEV, :] for t in tables], axis=0)
    got = jnp.dot(pick, table, preferred_element_type=F32)
    p = [got[:, q * 128 : (q + 1) * 128] for q in range(5)]
    low = lane_half(SLOTS_DEV)
    zero = jnp.zeros((SLOTS_DEV, 128), F32)
    fields = jnp.concatenate(
        [
            jnp.concatenate([p[0], p[1], jnp.where(low, p[2], zero)], axis=1),
            jnp.concatenate([join(p[2], p[3]), join(p[3], p[4]), jnp.where(low, swap(p[4]), zero)], axis=1),
        ],
        axis=0,
    ).astype(BF16)
    faces = jnp.dot(fields, sel_ref[...], preferred_element_type=F32)
    which = jnp.concatenate([far_ls, far_ls], axis=0)
    trace = jnp.zeros((2 * SLOTS_DEV, 128), F32)
    for face in range(6):
        trace = jnp.where(which == face, faces[:, face * 128 : (face + 1) * 128], trace)
    trace = jnp.concatenate([trace[:SLOTS_DEV], trace[SLOTS_DEV:]], axis=1).astype(BF16)
    rows = lax.broadcasted_iota(jnp.int32, (6 * E_DEV, SLOTS_DEV), 0)
    spread = jnp.where(rows == near_row, w, 0.0)
    flux = jnp.dot(jnp.concatenate(split(spread), axis=0), trace, preferred_element_type=F32)
    flux = flux[: 6 * E_DEV] + flux[6 * E_DEV :]
    weight_sum = jnp.sum(spread, axis=1, keepdims=True)
    lhs = jnp.concatenate(
        [
            jnp.concatenate(
                [flux[f * E_DEV : (f + 1) * E_DEV, :128], flux[f * E_DEV : (f + 1) * E_DEV, 128:]], axis=0
            )
            for f in range(6)
        ],
        axis=1,
    )
    lifted = jnp.dot(jnp.concatenate(split(lhs), axis=0), lift_ref[...], preferred_element_type=F32)
    lifted = lifted[: 2 * E_DEV] + lifted[2 * E_DEV :]
    coef = jnp.zeros((E_DEV, 384), F32)
    for f in range(6):
        coef = coef + weight_sum[f * E_DEV : (f + 1) * E_DEV] * inc_ref[f : f + 1, :]
    fields_own = vector_tiles(elem_ref[:E_DEV, :].astype(F32))
    for k in range(2):
        own = jnp.concatenate(fields_own[k][:3], axis=1)
        rows_k = slice(k * E_DEV, (k + 1) * E_DEV)
        out_ref[rows_k, :] = jac_ref[rows_k, :] + coef * own - lifted[rows_k]


def space_terms(quad, dev, far, near, cls, jac_terms, elem, tables):
    sel = np.zeros((384, 768), np.float32)
    sel[:DOF] = face_selector()
    vmem = pl.BlockSpec(memory_space=pltpu.VMEM)
    return pl.pallas_call(
        flux_kernel,
        out_shape=jax.ShapeDtypeStruct((2 * E_DEV, 384), F32),
        in_specs=[vmem] * (10 + len(tables)),
        out_specs=vmem,
        compiler_params=pltpu.CompilerParams(vmem_limit_bytes=12 * MIB),
        name="space_terms",
    )(
        quad.reshape(1, 16), dev, far, near, cls, jac_terms,
        jnp.asarray(sel, BF16), jnp.asarray(sel.T, BF16), jnp.asarray(face_incidence()), elem, *tables,
    )


def final_kernel(src_ref, time_ref, space_ref, res_ref, prod_ref, scratch):
    half = E_DEV // 2
    low = lane_half(half)
    for k, out_ref in enumerate((res_ref, prod_ref)):
        for q in range(3):
            scratch[q] = space_ref[k * E_DEV : (k + 1) * E_DEV, q * 128 : (q + 1) * 128]
        even = [scratch[q, pl.ds(0, half, stride=2), :] for q in range(3)]
        odd = [scratch[q, pl.ds(1, half, stride=2), :] for q in range(3)]
        tiles = [
            even[0],
            even[1],
            jnp.where(low, even[2], swap(odd[0])),
            join(odd[0], odd[1]),
            join(odd[1], odd[2]),
        ]
        for q in range(5):
            at = time_ref[pl.ds(k * ROWS + q, half, stride=5), :] + tiles[q]
            if k == 0:
                at = src_ref[pl.ds(q, half, stride=5), :] - at
            out_ref[pl.ds(q, half, stride=5), :] = at


def finish(source, time_parts, space):
    vmem = pl.BlockSpec(memory_space=pltpu.VMEM)
    return pl.pallas_call(
        final_kernel,
        out_shape=(jax.ShapeDtypeStruct((ROWS, 128), F32),) * 2,
        in_specs=[vmem] * 3,
        out_specs=(vmem, vmem),
        scratch_shapes=[pltpu.VMEM((3, E_DEV, 128), F32)],
        compiler_params=pltpu.CompilerParams(vmem_limit_bytes=4 * MIB),
        name="finish",
    )(source, time_parts, space)


def per_device(
    harmonic_state,
    direction,
    source,
    jacobian,
    frequency,
    viscosity,
    quad_weight,
    partner_device,
    partner_face,
    local_face,
    weight_index,
):
    coef = coefficients(frequency, viscosity)
    lin, elem = prep(coef, harmonic_state, direction)

    def over_space(x, turn):
        return lax.ppermute(x, "space", [(i, (i + turn) % N_SPACE) for i in range(N_SPACE)])

    across = over_space(elem, 4)
    received = lax.all_to_all(lin, "inst", 0, 0, tiled=True)
    pair = make_pair(elem, across)
    others = [over_space(pair, turn) for turn in (1, -1, 2)]
    back = spectral_sum(coef, received, pair)
    time_terms = lax.all_to_all(back, "inst", 0, 0, tiled=True)
    jac_terms = jacobian_product(jacobian, elem, back)
    space = space_terms(
        quad_weight,
        partner_device.reshape(1, SLOTS_DEV),
        partner_face,
        local_face,
        weight_index,
        jac_terms,
        elem,
        [pair] + others,
    )
    residual, product = finish(source.reshape(ROWS, 128), time_terms, space)
    return residual.reshape(1, FLAT), product.reshape(1, FLAT)


def solution(mesh):
    in_specs = (
        P("inst", "space"),
        P("inst", "space"),
        P("inst", "space"),
        P("inst", "space", None),
        P(),
        P(),
        P(),
        P("inst", "space", None),
        P("inst", "space"),
        P("inst", "space"),
        P("inst", "space"),
    )
    out_specs = (P("inst", "space"), P("inst", "space"))
    return jax.shard_map(
        per_device, mesh=mesh, in_specs=in_specs, out_specs=out_specs, check_vma=False
    )
```

```python
import jax
import jax.numpy as jnp
import numpy as np
from jax import lax
from jax.experimental import pallas as pl
from jax.experimental.pallas import tpu as pltpu
from jax.sharding import PartitionSpec as P

VARS = 5
PNODE = 4
E_DEV = 48
DOF = 320
SLOTS_DEV = 192
N_SPACE = 8
NT = 32
FLAT = E_DEV * DOF
ROWS = FLAT // 128
CHUNKS = 5
GROUPS = 16
BLOCK = 16
PIECE = GROUPS * 4 * DOF
SPARE = 16
MIB = 1024 * 1024
F32 = jnp.float32
BF16 = jnp.bfloat16


def face_selector():
    table = np.zeros((DOF, 6 * 128), np.float32)
    for face in range(6):
        fixed = 0 if face % 2 == 0 else PNODE - 1
        for comp in range(VARS):
            for first in range(PNODE):
                for second in range(PNODE):
                    if face < 2:
                        i, j, k = fixed, first, second
                    elif face < 4:
                        i, j, k = first, fixed, second
                    else:
                        i, j, k = first, second, fixed
                    table[comp * 64 + i * 16 + j * 4 + k, face * 128 + comp * 16 + first * 4 + second] = 1.0
    return table


def face_incidence():
    rows = np.zeros((8, 384), np.float32)
    for face in range(6):
        rows[face, :DOF] = face_selector()[:, face * 128 : (face + 1) * 128].sum(axis=1)
    return rows


def lane_half(rows):
    return lax.broadcasted_iota(jnp.int32, (rows, 128), 1) < 64


def swap(x):
    return pltpu.roll(x, 64, 1)


def join(low, high):
    return jnp.where(lane_half(low.shape[0]), swap(low), swap(high))


def circulant_parts():
    j = np.arange(1, NT)
    sign = 1.0 - 2.0 * (j % 2)
    angle = np.pi * j / NT
    first = np.concatenate([[0.0], 0.5 * sign * np.cos(angle) / np.sin(angle)])
    second = np.concatenate([[-(NT * NT + 2) / 12.0], -sign / (2.0 * np.sin(angle) ** 2)])
    return first, second


def coef_kernel(freq_ref, visc_ref, coef_ref):
    first, second = circulant_parts()
    freq, visc = freq_ref[0], visc_ref[0]
    half = NT // 2
    for part, sgn in enumerate((1.0, -1.0)):
        for j in range(half):
            a = 0.5 * (first[j] + sgn * first[j + half])
            b = 0.5 * (second[j] + sgn * second[j + half])
            row = part * half + j
            coef_ref[row : row + 1, :] = jnp.full((1, 128), freq * float(a) + visc * float(b), F32)


def coefficients(frequency, viscosity):
    smem = pl.BlockSpec(memory_space=pltpu.SMEM)
    return pl.pallas_call(
        coef_kernel,
        out_shape=jax.ShapeDtypeStruct((NT, 128), F32),
        in_specs=[smem, smem],
        out_specs=pl.BlockSpec(memory_space=pltpu.VMEM),
        compiler_params=pltpu.CompilerParams(vmem_limit_bytes=MIB),
        cost_estimate=pl.CostEstimate(flops=4 * 10**9, bytes_accessed=0, transcendentals=0),
        name="coefficients",
    )(frequency, viscosity)


def prep_kernel(mark_ref, s_ref, d_ref, lin_ref, elem_ref, flat, wide):
    for k, ref in enumerate((s_ref, d_ref)):
        for r in range(ROWS):
            flat[k * ROWS + r : k * ROWS + r + 1, :] = ref[0:1, r * 128 : (r + 1) * 128].astype(F32)
    flat[2 * ROWS : 256, :] = jnp.zeros((256 - 2 * ROWS, 128), F32)
    lin_ref[...] = flat[...].astype(BF16)
    half = E_DEV // 2
    low = lane_half(half)
    s = [flat[pl.ds(q, half, stride=5), :] for q in range(5)]
    d = [flat[pl.ds(ROWS + q, half, stride=5), :] for q in range(5)]
    even = [s[0], s[1], jnp.where(low, s[2], swap(d[0])), join(d[0], d[1]), join(d[1], d[2])]
    odd = [join(s[2], s[3]), join(s[3], s[4]), jnp.where(low, swap(s[4]), d[2]), d[3], d[4]]
    for q in range(5):
        wide[q, pl.ds(0, half, stride=2), :] = even[q]
        wide[q, pl.ds(1, half, stride=2), :] = odd[q]
    for q in range(5):
        elem_ref[:E_DEV, q * 128 : (q + 1) * 128] = wide[q].astype(BF16)
    elem_ref[E_DEV:, :] = jnp.zeros((SPARE // 2, 2 * DOF), BF16)


def prep(mark, state, direction):
    vmem = pl.BlockSpec(memory_space=pltpu.VMEM)
    return pl.pallas_call(
        prep_kernel,
        out_shape=(
            jax.ShapeDtypeStruct((256, 128), BF16),
            jax.ShapeDtypeStruct((E_DEV + SPARE // 2, 2 * DOF), BF16),
        ),
        in_specs=[pl.BlockSpec(memory_space=pl.ANY), vmem, vmem],
        out_specs=(vmem, vmem),
        scratch_shapes=[pltpu.VMEM((256, 128), F32), pltpu.VMEM((5, E_DEV, 128), F32)],
        compiler_params=pltpu.CompilerParams(vmem_limit_bytes=4 * MIB),
        name="prep",
    )(mark, state, direction)


def pair_kernel(own_ref, across_ref, after_ref, pair_ref):
    pair_ref[:E_DEV, :] = own_ref[:E_DEV, :]
    pair_ref[E_DEV : 2 * E_DEV, :] = across_ref[:E_DEV, :]
    pair_ref[2 * E_DEV :, :] = jnp.zeros((SPARE, 2 * DOF), BF16)


def make_pair(own, across, after):
    vmem = pl.BlockSpec(memory_space=pltpu.VMEM)
    return pl.pallas_call(
        pair_kernel,
        out_shape=jax.ShapeDtypeStruct((2 * E_DEV + SPARE, 2 * DOF), BF16),
        in_specs=[vmem, vmem, pl.BlockSpec(memory_space=pl.ANY)],
        out_specs=vmem,
        compiler_params=pltpu.CompilerParams(vmem_limit_bytes=2 * MIB),
        name="pair",
    )(own, across, after)


def spectral_kernel(coef_ref, x_ref, after_ref, y_ref):
    half = NT // 2
    x = x_ref[...].astype(F32).reshape(NT, 8, 128)

    def part(sgn):
        base = 0 if sgn > 0 else half
        c = [jnp.broadcast_to(coef_ref[base + j : base + j + 1, :], (8, 128)) for j in range(half)]
        u = [x[s] + sgn * x[s + half] for s in range(half)]
        out = []
        for t in range(half):
            acc = None
            for s in range(half):
                j = t - s
                term = c[j % half] * u[s]
                if acc is None:
                    acc = term
                elif j < 0 and sgn < 0:
                    acc = acc - term
                else:
                    acc = acc + term
            out.append(acc)
        return out

    even = part(1.0)
    for t in range(half):
        y_ref[t * 8 : (t + 1) * 8, :] = even[t]
    odd = part(-1.0)
    for t in range(half):
        e = y_ref[t * 8 : (t + 1) * 8, :]
        y_ref[t * 8 : (t + 1) * 8, :] = e + odd[t]
        y_ref[(t + half) * 8 : (t + half + 1) * 8, :] = e - odd[t]


def spectral_sum(coef, received, after):
    vmem = pl.BlockSpec(memory_space=pltpu.VMEM)
    return pl.pallas_call(
        spectral_kernel,
        out_shape=jax.ShapeDtypeStruct((256, 128), F32),
        in_specs=[vmem] * 2 + [pl.BlockSpec(memory_space=pl.ANY)],
        out_specs=vmem,
        compiler_params=pltpu.CompilerParams(vmem_limit_bytes=4 * MIB),
        cost_estimate=pl.CostEstimate(flops=10**10, bytes_accessed=0, transcendentals=0),
        name="spectral",
    )(coef, received, after)


def vector_tiles(elem):
    p = [elem[:, q * 128 : (q + 1) * 128] for q in range(5)]
    low = lane_half(E_DEV)
    zero = jnp.zeros((E_DEV, 128), F32)
    s = [p[0], p[1], jnp.where(low, p[2], zero), jnp.where(low, zero, swap(p[0])), join(p[0], p[1]), join(p[1], p[2])]
    d = [join(p[2], p[3]), join(p[3], p[4]), jnp.where(low, swap(p[4]), zero), jnp.where(low, zero, p[2]), p[3], p[4]]
    return s, d


def jacobian_kernel(jac_hbm, elem_ref, after_ref, out_ref, held, weights, acc, rows, sems):
    def piece(c, start):
        return pltpu.make_async_copy(jac_hbm.at[0, :, pl.ds(start, PIECE)], held.at[c], sems.at[c])

    for c in range(CHUNKS):
        piece(c, c * PIECE).start()
    s, d = vector_tiles(elem_ref[:E_DEV, :].astype(F32))
    pad = jnp.zeros((128 - 2 * E_DEV, 128), F32)
    blocks = E_DEV // BLOCK
    turned = []
    for q in range(3):
        parts = []
        for b in range(blocks):
            parts += [s[q][b * BLOCK : (b + 1) * BLOCK], d[q][b * BLOCK : (b + 1) * BLOCK]]
        turned.append(jnp.concatenate(parts + [pad], axis=0).T)
    turned = jnp.concatenate(turned, axis=0)[:DOF]
    lane = lax.broadcasted_iota(jnp.int32, (DOF, 128), 1)
    for b in range(blocks):
        for i in range(4):
            at = turned if i == b else pltpu.roll(turned, (i - b) * 32 % 128, 1)
            at = jnp.where((lane >= 32 * i) & (lane < 32 * (i + 1)), at, 0.0)
            weights[b, DOF * i : DOF * (i + 1), :] = at.astype(BF16)
    e = lax.broadcasted_iota(jnp.int32, (BLOCK, 128), 0)
    keep = (lax.broadcasted_iota(jnp.int32, (BLOCK, 128), 1) & (BLOCK - 1)) == e

    def step(c, carry):
        piece(c, pl.multiple_of(c * PIECE, PIECE)).wait()
        for b in range(blocks):
            lhs = jnp.concatenate(
                [
                    held[c, b * BLOCK : (b + 1) * BLOCK, g * 4 * DOF : (g + 1) * 4 * DOF]
                    for g in range(GROUPS)
                ],
                axis=0,
            )
            res = jnp.dot(lhs, weights[b], preferred_element_type=F32)
            res = jnp.where(keep[None], res.reshape(GROUPS, BLOCK, 128), 0.0)
            acc[b, pl.ds(pl.multiple_of(c * GROUPS, GROUPS), GROUPS), :] = jnp.sum(res, axis=1)
        return carry

    lax.fori_loop(0, CHUNKS, step, 0)
    groups = CHUNKS * GROUPS
    lane = lax.broadcasted_iota(jnp.int32, (groups, 128), 1)
    for i in range(4):
        at = jnp.zeros((groups, 128), F32)
        for b in range(blocks):
            moved = acc[b] if i == b else pltpu.roll(acc[b], (b - i) * 32 % 128, 1)
            at = jnp.where((lane >= 32 * b) & (lane < 32 * (b + 1)), moved, at)
        rows[pl.ds(i, groups, stride=4), :] = at
    rows[DOF:, :] = jnp.zeros((384 - DOF, 128), F32)
    for q in range(3):
        back = rows[q * 128 : (q + 1) * 128, :].T
        for b in range(blocks):
            for k in range(2):
                out_ref[k * E_DEV + b * BLOCK : k * E_DEV + (b + 1) * BLOCK, q * 128 : (q + 1) * 128] = back[
                    b * 32 + k * BLOCK : b * 32 + (k + 1) * BLOCK
                ]


def jacobian_product(jacobian, elem, after):
    return pl.pallas_call(
        jacobian_kernel,
        out_shape=jax.ShapeDtypeStruct((2 * E_DEV, 384), F32),
        in_specs=[
            pl.BlockSpec(memory_space=pltpu.HBM),
            pl.BlockSpec(memory_space=pltpu.VMEM),
            pl.BlockSpec(memory_space=pl.ANY),
        ],
        out_specs=pl.BlockSpec(memory_space=pltpu.VMEM),
        scratch_shapes=[
            pltpu.VMEM((CHUNKS, E_DEV, PIECE), BF16),
            pltpu.VMEM((E_DEV // BLOCK, 4 * DOF, 128), BF16),
            pltpu.VMEM((E_DEV // BLOCK, CHUNKS * GROUPS, 128), F32),
            pltpu.VMEM((384, 128), F32),
            pltpu.SemaphoreType.DMA((CHUNKS,)),
        ],
        compiler_params=pltpu.CompilerParams(vmem_limit_bytes=49 * MIB),
        cost_estimate=pl.CostEstimate(
            flops=2 * 2 * E_DEV * DOF * DOF * 48, bytes_accessed=2 * E_DEV * DOF * DOF, transcendentals=0
        ),
        name="jacobian",
    )(jacobian, elem, after)


def split(x):
    high = x.astype(BF16)
    return high, (x - high.astype(F32)).astype(BF16)


def flux_kernel(
    quad_ref, dev_ref, far_ref, near_ref, cls_ref, jac_ref, sel_ref, lift_ref, inc_ref, elem_ref, *rest
):
    tables, out_ref = rest[:-1], rest[-1]
    me = lax.axis_index("space")
    far = far_ref[...]
    near = near_ref[...]
    cls = cls_ref[...]
    far_e = (far * 10923) >> 16
    far_l = far - far_e * 6
    near_e = (near * 10923) >> 16
    near_row = (near - near_e * 6) * E_DEV + near_e
    turn = (dev_ref[...] - me) & (N_SPACE - 1)
    block = jnp.zeros((1, SLOTS_DEV), jnp.int32)
    for at, which in enumerate((0, 4, 7, 3, 6, 2, 1, 5)):
        block = jnp.where(turn == which, at, block)
    column = block * E_DEV + far_e
    w = jnp.zeros((1, SLOTS_DEV), F32)
    for c in range(16):
        w = jnp.where(cls == c, quad_ref[:, c : c + 1], w)
    r = lax.broadcasted_iota(jnp.int32, (SLOTS_DEV, SLOTS_DEV), 0)
    c = lax.broadcasted_iota(jnp.int32, (SLOTS_DEV, SLOTS_DEV), 1)
    both = (far_l * 512 + column).astype(F32)
    code = jnp.sum(jnp.where(r == c, both, 0.0), axis=1, keepdims=True).astype(jnp.int32)
    column_s = code & 511
    far_ls = code >> 9
    total = N_SPACE * E_DEV
    pick = (lax.broadcasted_iota(jnp.int32, (SLOTS_DEV, total), 1) == column_s).astype(F32).astype(BF16)
    table = jnp.concatenate([t[: (2 if at < 3 else 1) * E_DEV, :] for at, t in enumerate(tables)], axis=0)
    got = jnp.dot(pick, table, preferred_element_type=F32)
    p = [got[:, q * 128 : (q + 1) * 128] for q in range(5)]
    low = lane_half(SLOTS_DEV)
    zero = jnp.zeros((SLOTS_DEV, 128), F32)
    fields = jnp.concatenate(
        [
            jnp.concatenate([p[0], p[1], jnp.where(low, p[2], zero)], axis=1),
            jnp.concatenate([join(p[2], p[3]), join(p[3], p[4]), jnp.where(low, swap(p[4]), zero)], axis=1),
        ],
        axis=0,
    ).astype(BF16)
    faces = jnp.dot(fields, sel_ref[...], preferred_element_type=F32)
    which = jnp.concatenate([far_ls, far_ls], axis=0)
    trace = jnp.zeros((2 * SLOTS_DEV, 128), F32)
    for face in range(6):
        trace = jnp.where(which == face, faces[:, face * 128 : (face + 1) * 128], trace)
    trace = jnp.concatenate([trace[:SLOTS_DEV], trace[SLOTS_DEV:]], axis=1).astype(BF16)
    rows = lax.broadcasted_iota(jnp.int32, (6 * E_DEV, SLOTS_DEV), 0)
    spread = jnp.where(rows == near_row, w, 0.0)
    flux = jnp.dot(jnp.concatenate(split(spread), axis=0), trace, preferred_element_type=F32)
    flux = flux[: 6 * E_DEV] + flux[6 * E_DEV :]
    weight_sum = jnp.sum(spread, axis=1, keepdims=True)
    lhs = jnp.concatenate(
        [
            jnp.concatenate(
                [flux[f * E_DEV : (f + 1) * E_DEV, :128], flux[f * E_DEV : (f + 1) * E_DEV, 128:]], axis=0
            )
            for f in range(6)
        ],
        axis=1,
    )
    lifted = jnp.dot(jnp.concatenate(split(lhs), axis=0), lift_ref[...], preferred_element_type=F32)
    lifted = lifted[: 2 * E_DEV] + lifted[2 * E_DEV :]
    coef = jnp.zeros((E_DEV, 384), F32)
    for f in range(6):
        coef = coef + weight_sum[f * E_DEV : (f + 1) * E_DEV] * inc_ref[f : f + 1, :]
    fields_own = vector_tiles(elem_ref[:E_DEV, :].astype(F32))
    for k in range(2):
        own = jnp.concatenate(fields_own[k][:3], axis=1)
        rows_k = slice(k * E_DEV, (k + 1) * E_DEV)
        out_ref[rows_k, :] = jac_ref[rows_k, :] + coef * own - lifted[rows_k]


def space_terms(quad, dev, far, near, cls, jac_terms, elem, tables):
    sel = np.zeros((384, 768), np.float32)
    sel[:DOF] = face_selector()
    vmem = pl.BlockSpec(memory_space=pltpu.VMEM)
    return pl.pallas_call(
        flux_kernel,
        out_shape=jax.ShapeDtypeStruct((2 * E_DEV, 384), F32),
        in_specs=[vmem] * (10 + len(tables)),
        out_specs=vmem,
        compiler_params=pltpu.CompilerParams(vmem_limit_bytes=12 * MIB),
        name="space_terms",
    )(
        quad.reshape(1, 16), dev, far, near, cls, jac_terms,
        jnp.asarray(sel, BF16), jnp.asarray(sel.T, BF16), jnp.asarray(face_incidence()), elem, *tables,
    )


def final_kernel(src_ref, time_ref, space_ref, res_ref, prod_ref, scratch):
    half = E_DEV // 2
    low = lane_half(half)
    for k, out_ref in enumerate((res_ref, prod_ref)):
        for q in range(3):
            scratch[q] = space_ref[k * E_DEV : (k + 1) * E_DEV, q * 128 : (q + 1) * 128]
        even = [scratch[q, pl.ds(0, half, stride=2), :] for q in range(3)]
        odd = [scratch[q, pl.ds(1, half, stride=2), :] for q in range(3)]
        tiles = [
            even[0],
            even[1],
            jnp.where(low, even[2], swap(odd[0])),
            join(odd[0], odd[1]),
            join(odd[1], odd[2]),
        ]
        for q in range(5):
            at = time_ref[pl.ds(k * ROWS + q, half, stride=5), :] + tiles[q]
            if k == 0:
                at = src_ref[pl.ds(q, half, stride=5), :] - at
            out_ref[pl.ds(q, half, stride=5), :] = at


def finish(source, time_parts, space):
    vmem = pl.BlockSpec(memory_space=pltpu.VMEM)
    return pl.pallas_call(
        final_kernel,
        out_shape=(jax.ShapeDtypeStruct((ROWS, 128), F32),) * 2,
        in_specs=[vmem] * 3,
        out_specs=(vmem, vmem),
        scratch_shapes=[pltpu.VMEM((3, E_DEV, 128), F32)],
        compiler_params=pltpu.CompilerParams(vmem_limit_bytes=4 * MIB),
        name="finish",
    )(source, time_parts, space)


def per_device(
    harmonic_state,
    direction,
    source,
    jacobian,
    frequency,
    viscosity,
    quad_weight,
    partner_device,
    partner_face,
    local_face,
    weight_index,
):
    coef = coefficients(frequency, viscosity)
    lin, elem = prep(coef, harmonic_state, direction)

    def over_space(x, turn):
        return lax.ppermute(x, "space", [(i, (i + turn) % N_SPACE) for i in range(N_SPACE)])

    right = over_space(elem, -1)
    across = over_space(elem, 4)
    received = lax.all_to_all(lin, "inst", 0, 0, tiled=True)
    pair = make_pair(elem, across, right)
    others = [over_space(pair, 1), over_space(pair, 2), right, over_space(elem, 3)]
    back = spectral_sum(coef, received, pair)
    time_terms = lax.all_to_all(back, "inst", 0, 0, tiled=True)
    jac_terms = jacobian_product(jacobian, elem, back)
    space = space_terms(
        quad_weight,
        partner_device.reshape(1, SLOTS_DEV),
        partner_face,
        local_face,
        weight_index,
        jac_terms,
        elem,
        [pair] + others,
    )
    residual, product = finish(source.reshape(ROWS, 128), time_terms, space)
    return residual.reshape(1, FLAT), product.reshape(1, FLAT)


def solution(mesh):
    in_specs = (
        P("inst", "space"),
        P("inst", "space"),
        P("inst", "space"),
        P("inst", "space", None),
        P(),
        P(),
        P(),
        P("inst", "space", None),
        P("inst", "space"),
        P("inst", "space"),
        P("inst", "space"),
    )
    out_specs = (P("inst", "space"), P("inst", "space"))
    return jax.shard_map(
        per_device, mesh=mesh, in_specs=in_specs, out_specs=out_specs, check_vma=False
    )
```
